32 devices in a mesh: seq: 16 (over z, y, x), tp: 2 (over core).
Axes of the slice: x: 2, y: 2, z: 4, core: 2. Of those that a mesh axis runs over, the one named last changes fastest.
Arguments:
- tokens: bfloat16 [8192, 2048], P('seq', 'tp'), may hold values from -6 to 6
- in_weight: bfloat16 [2048, 2, 2048], P(None, None, 'tp'), may hold values from -0.125 to 0.125
- bc_weight: bfloat16 [2048, 256], P(None, 'tp'), may hold values from -0.125 to 0.125
- dt_weight: bfloat16 [2, 2048, 32], P(None, None, 'tp'), may hold values from -0.125 to 0.125
- dt_bias: float32 [2, 32], P(None, 'tp'), may hold values from -2 to 0.5
- decay_rate: float32 [32], P('tp'), may hold values from 1e-05 to 0.5
- skip_gain: float32 [32], P('tp'), may hold values from 0.5 to 300
- out_weight: bfloat16 [2048, 2048], P('tp'), may hold values from -0.1875 to 0.1875
Outputs:
- mixed: bfloat16 [8192, 2048], P('seq', 'tp')
The draws below stay inside these ranges and needn't reach their ends.
All inputs are finite; a program needn't handle non-finite values.
Results may differ from the reference program's by a relative error of at most 0.018.
Values may be sent and summed in bfloat16 or wider, within the bound.
A program may use at most 128 MiB of HBM per device.

```python
import math
import jax
import jax.numpy as jnp
from jax import lax

D = 2048
HEADS = 32
HEAD_DIM = 64
STATE = 128
TOK_DEV = 512
TOKENS = 8192
CHANNELS = 2048
N_SEQ = 16
N_TP = 2


def draw_decay_rate(key, part):
    key = jax.random.fold_in(key, 11)
    pick_key, slow_key, fast_key = jax.random.split(key, 3)
    share = 0.5
    slow_pick = jax.random.uniform(pick_key, (HEADS,), jnp.float32) < share
    slow_rate = jnp.exp(jax.random.uniform(slow_key, (HEADS,), jnp.float32, math.log(1e-05), math.log(0.0002)))
    fast_rate = jnp.exp(jax.random.uniform(fast_key, (HEADS,), jnp.float32, math.log(0.02), math.log(0.5)))
    return jnp.where(slow_pick, slow_rate, fast_rate).astype(jnp.float32)


def draw_skip_gain(key, part):
    key = jax.random.fold_in(key, 13)
    low_key = jax.random.fold_in(key, 1)
    gain = jnp.exp(jax.random.uniform(low_key, (HEADS,), jnp.float32, math.log(0.5), math.log(300.0)))
    return gain.astype(jnp.float32)


def with_spikes(drawn, key, source, target, parts, factor):
    def block_of(position):
        return (jnp.arange(drawn.shape[position]) // (drawn.shape[position] // parts)).reshape((-1,) + (1,) * (drawn.ndim - 1 - position))

    near = jax.random.permutation(key, parts)[block_of(target)]
    second = (block_of(target) + parts // 2) % parts
    return jnp.where((block_of(source) == near) | (block_of(source) == second), factor * drawn, drawn)


def steps_of(key, extent, cuts, least, top_value):
    def one(position, blocks):
        steps = jax.random.uniform(jax.random.fold_in(jax.random.fold_in(key, 6), position), (blocks,), jnp.float32, least / len(cuts), top_value / len(cuts))
        return jnp.repeat(jnp.exp(steps), extent[position] // blocks).reshape((-1,) + (1,) * (len(extent) - position - 1))

    level = one(*cuts[0])
    for cut in cuts[1:]:
        level = level * one(*cut)
    return level


def bell_draw(stream_key, shape, scale, bound, cuts=(), kind=jnp.bfloat16):
    factor_of = steps_of(stream_key, shape, cuts, -0.22, 0.18) if cuts else 1.0
    entries = jax.random.normal(stream_key, shape, jnp.float32) * scale * factor_of
    return jnp.minimum(jnp.maximum(entries, -bound), bound).astype(kind)


def bell_draw_with(own_key, extent, scale, limit, cuts, heavy, kind=jnp.bfloat16):
    drawn = scale * jax.random.normal(own_key, extent, jnp.float32)
    if cuts:
        drawn = drawn * steps_of(own_key, extent, cuts, -0.22, 0.18)
    return jnp.clip(with_spikes(drawn, jax.random.fold_in(own_key, 3), *heavy), -limit, limit).astype(kind)


def setup_inputs(seed: int = 0) -> dict:
    seeds = jax.random.split(jax.random.key(seed), 9)
    tokens = bell_draw(seeds[0], (TOKENS, D), 1.0, 6.0, ((0, 16), (1, 2)))
    in_weight = bell_draw(seeds[1], (D, 2, CHANNELS), D ** -0.5, 0.125, ((2, 2),))
    bc_weight = bell_draw(seeds[2], (D, 2 * STATE), D ** -0.5, 0.125, ((1, 2),))
    dt_weight = bell_draw(seeds[3], (2, D, HEADS), D ** -0.5, 0.125, ((2, 2),))
    dt_bias = jnp.clip(-2.0 + 2.5 * jax.random.uniform(seeds[4], (2, HEADS), jnp.float32) ** steps_of(seeds[4], (2, HEADS), ((1, 2),), -0.2, 0.2), -2.0, 0.5)
    decay_rate = draw_decay_rate(jax.random.fold_in(seeds[8], 71), 0)
    skip_gain = draw_skip_gain(jax.random.fold_in(seeds[8], 71), 0)
    out_weight = bell_draw_with(seeds[7], (CHANNELS, D), CHANNELS ** -0.5, 0.1875, ((0, 2),), (0, 1, 2, 2.0))
    return {"tokens": tokens, "in_weight": in_weight, "bc_weight": bc_weight, "dt_weight": dt_weight, "dt_bias": dt_bias, "decay_rate": decay_rate, "skip_gain": skip_gain, "out_weight": out_weight}


def block_terms(values, keys, queries, forward_steps, backward_steps, decay_rate):
    length = values.shape[0]
    forward_logs = -decay_rate[None, :] * forward_steps
    backward_logs = -decay_rate[None, :] * backward_steps
    forward_upto = jnp.cumsum(forward_logs, axis=0)
    forward_before = forward_upto - forward_logs
    backward_upto = jnp.cumsum(backward_logs, axis=0)
    backward_before = backward_upto - backward_logs
    forward_total = forward_upto[-1]
    backward_total = backward_upto[-1]
    scores = jnp.dot(queries, keys.T, preferred_element_type=jnp.float32)
    rows = jnp.arange(length, dtype=jnp.int32)[:, None]
    cols = jnp.arange(length, dtype=jnp.int32)[None, :]
    lower_mask = (rows > cols)[None]
    upper_mask = (rows < cols)[None]
    forward_gap = jnp.where(lower_mask, forward_before.T[:, :, None] - forward_upto.T[:, None, :], 0.0)
    forward_weights = jnp.where(lower_mask, scores[None] * jnp.exp(forward_gap) * forward_steps.T[:, None, :], 0.0).astype(jnp.bfloat16)
    backward_gap = jnp.where(upper_mask, backward_before.T[:, None, :] - backward_upto.T[:, :, None], 0.0)
    backward_weights = jnp.where(upper_mask, scores[None] * jnp.exp(backward_gap) * backward_steps.T[:, None, :], 0.0).astype(jnp.bfloat16)
    values_wide = values.astype(jnp.float32)
    inner = jnp.einsum('hts,shp->thp', forward_weights.astype(jnp.float32), values_wide)
    inner = inner + jnp.einsum('hts,shp->thp', backward_weights.astype(jnp.float32), values_wide)
    keys_wide = keys.astype(jnp.float32)
    forward_keys = (keys_wide[:, None, :] * (jnp.exp(forward_total[None, :] - forward_upto) * forward_steps)[:, :, None]).astype(jnp.bfloat16)
    backward_keys = (keys_wide[:, None, :] * (jnp.exp(backward_before) * backward_steps)[:, :, None]).astype(jnp.bfloat16)
    forward_state = jnp.einsum('shp,shn->hpn', values_wide, forward_keys.astype(jnp.float32))
    backward_state = jnp.einsum('shp,shn->hpn', values_wide, backward_keys.astype(jnp.float32))
    return (inner, forward_state, backward_state, forward_total, backward_total, forward_before, backward_upto)

def reference(tokens, in_weight, bc_weight, dt_weight, dt_bias, decay_rate, skip_gain, out_weight):
    tokens_wide = tokens.astype(jnp.float32)
    projected = jnp.einsum('td,dkf->tkf', tokens_wide, in_weight.astype(jnp.float32))
    values = projected[:, 0].astype(jnp.bfloat16).reshape(N_SEQ, TOK_DEV, HEADS, HEAD_DIM)
    gates = projected[:, 1].reshape(N_SEQ, TOK_DEV, HEADS, HEAD_DIM)
    both = jnp.dot(tokens, bc_weight, preferred_element_type=jnp.float32).astype(jnp.bfloat16)
    keys = both[:, :STATE].reshape(N_SEQ, TOK_DEV, STATE)
    queries = both[:, STATE:].reshape(N_SEQ, TOK_DEV, STATE)
    steps = jax.nn.softplus(jnp.einsum('td,kdh->kth', tokens_wide, dt_weight.astype(jnp.float32)) + dt_bias[:, None, :])
    forward_steps = steps[0].reshape(N_SEQ, TOK_DEV, HEADS)
    backward_steps = steps[1].reshape(N_SEQ, TOK_DEV, HEADS)
    results = lax.map(lambda items: block_terms(items[0], items[1], items[2], items[3], items[4], decay_rate), (values, keys, queries, forward_steps, backward_steps))
    inner, forward_state, backward_state, forward_total, backward_total, forward_before, backward_upto = results

    def carry_on(carry, items):
        state, total = items
        return (jnp.exp(total)[:, None, None] * carry + state, carry)
    zeros_state = jnp.zeros((HEADS, HEAD_DIM, STATE), jnp.float32)
    forward_enter = lax.scan(carry_on, zeros_state, (forward_state, forward_total))[1]
    backward_enter = lax.scan(carry_on, zeros_state, (backward_state, backward_total), reverse=True)[1]
    queries_wide = queries.astype(jnp.float32)
    mix = inner + jnp.exp(forward_before)[..., None] * jnp.einsum('btn,bhpn->bthp', queries_wide, forward_enter, precision=lax.Precision.HIGHEST)
    mix = mix + jnp.exp(backward_total[:, None, :] - backward_upto)[..., None] * jnp.einsum('btn,bhpn->bthp', queries_wide, backward_enter, precision=lax.Precision.HIGHEST)
    mix = mix + skip_gain[None, None, :, None] * values.astype(jnp.float32)
    gated = mix * jax.nn.silu(gates)
    power = lax.optimization_barrier(jnp.mean(gated * gated, axis=-1, keepdims=True))
    hidden = (gated * lax.rsqrt(power + 1e-05)).astype(jnp.bfloat16).reshape(TOKENS, CHANNELS)
    group = CHANNELS // N_TP

    def add_group(index, total):
        part_rows = lax.dynamic_slice_in_dim(hidden, (index * group).astype(jnp.int32), group, 1)
        part_weight = lax.dynamic_slice_in_dim(out_weight, (index * group).astype(jnp.int32), group, 0)
        rounded = jnp.dot(part_rows, part_weight, preferred_element_type=jnp.float32).astype(jnp.bfloat16)
        rounded = lax.optimization_barrier(rounded)
        return total + rounded.astype(jnp.float32)
    total = lax.fori_loop(0, N_TP, add_group, jnp.zeros((TOKENS, D), jnp.float32))
    return total.astype(jnp.bfloat16)
```

```python
import functools

import jax
import jax.numpy as jnp
from jax import lax
from jax.experimental import pallas as pl
from jax.experimental.pallas import tpu as pltpu
from jax.sharding import PartitionSpec as P

HEAD_DIM = 64
STATE = 128
CHUNK = 128
GROUP = 4
VMEM_LIMIT = 48 * 1024 * 1024
F32 = jnp.float32
BF16 = jnp.bfloat16
HIGH = lax.Precision.HIGHEST


def dot(a, b, contract=((1,), (0,)), precision=None):
    return lax.dot_general(
        a, b, (contract, ((), ())), precision=precision, preferred_element_type=F32
    )


def split_wide(value):
    high = value.astype(BF16)
    return jnp.concatenate([high, (value - high.astype(F32)).astype(BF16)], axis=1)


def spread_matrix(count, dtype, copies=1):
    rows = lax.broadcasted_iota(jnp.int32, (copies * count, count * HEAD_DIM), 0)
    lanes = lax.broadcasted_iota(jnp.int32, (copies * count, count * HEAD_DIM), 1)
    return (lax.rem(rows, count) == lanes // HEAD_DIM).astype(dtype)


def chunk_decays(raw, rate):
    steps = jnp.maximum(raw, 0.0) + jnp.log1p(jnp.exp(-jnp.abs(raw)))
    logs = -rate * steps
    rows = lax.broadcasted_iota(jnp.int32, (CHUNK, CHUNK), 0)
    cols = lax.broadcasted_iota(jnp.int32, (CHUNK, CHUNK), 1)
    running = (rows >= cols).astype(F32)
    upto = dot(running, logs, precision=HIGH)
    return steps, upto, upto - logs


def states_kernel(proj_ref, both_ref, raw_ref, rate_ref, local_ref, send_ref, total_ref, sums):
    heads2 = raw_ref.shape[1]
    heads = heads2 // 2
    width = heads * HEAD_DIM
    chunks = raw_ref.shape[0] // CHUNK
    spread = spread_matrix(heads2, BF16, 2)
    spread_wide = spread_matrix(heads2, F32)
    forward = lax.broadcasted_iota(jnp.int32, (CHUNK, heads2), 1) < heads
    totals = []
    for c in range(chunks):
        rows = pl.ds(c * CHUNK, CHUNK)
        steps, upto, before = chunk_decays(raw_ref[rows, :], rate_ref[...])
        last = upto[CHUNK - 1 : CHUNK, :]
        weight = jnp.exp(jnp.where(forward, last - upto, before)) * steps
        weight = dot(split_wide(weight), spread)
        values = proj_ref[0, rows, :].astype(BF16).astype(F32)
        weighted = (jnp.concatenate([values, values], axis=1) * weight).astype(BF16)
        sums[c] = dot(both_ref[rows, :STATE], weighted, ((0,), (0,)))
        totals.append(dot(jnp.broadcast_to(last, (8, heads2)), spread_wide, precision=HIGH))
    block = functools.reduce(jnp.add, totals)
    quarter = width // GROUP
    for way in range(2):
        side = slice(way * width, (way + 1) * width)
        order = range(chunks) if way == 0 else range(chunks - 1, -1, -1)
        carry = jnp.zeros((STATE, width), F32)
        for c in order:
            local_ref[c, :, side] = carry.astype(BF16)
            carry = jnp.exp(totals[c][:1, side]) * carry + sums[c, :, side]
        for g in range(GROUP):
            part = slice(g * quarter, (g + 1) * quarter)
            send_ref[g, way] = carry[:, part].astype(BF16)
            total_ref[g, way] = block[:, side][:, part]


def carry_kernel(
    outer,
    send_ref,
    total_ref,
    enter_ref,
    got,
    got_total,
    inner,
    group,
    group_total,
    far,
    far_total,
    back,
    landed,
    send1,
    recv1,
    send2,
    recv2,
    send3,
    recv3,
):
    seq = lax.axis_index("seq")
    z, g = seq // GROUP, seq % GROUP

    def peer(zz, gg):
        return {"seq": zz * GROUP + gg}

    barrier = pltpu.get_barrier_semaphore()
    for d in range(1, GROUP):
        pl.semaphore_signal(
            barrier, inc=1, device_id=peer(z, (g + d) % GROUP), device_id_type=pl.DeviceIdType.MESH
        )
    for d in range(1, outer):
        pl.semaphore_signal(
            barrier, inc=1, device_id=peer((z + d) % outer, g), device_id_type=pl.DeviceIdType.MESH
        )
    pl.semaphore_wait(barrier, GROUP - 1 + outer - 1)

    def push(source, target, sends, recvs, slot, where):
        copy = pltpu.make_async_remote_copy(
            src_ref=source,
            dst_ref=target,
            send_sem=sends.at[slot],
            recv_sem=recvs.at[slot],
            device_id=where,
            device_id_type=pl.DeviceIdType.MESH,
        )
        copy.start()
        return copy

    copies = []
    for d in range(1, GROUP):
        to = (g + d) % GROUP
        copies.append(push(total_ref.at[to], got_total.at[g], send1, recv1, 2 * d - 1, peer(z, to)))
        copies.append(push(send_ref.at[to], got.at[g], send1, recv1, 2 * d - 2, peer(z, to)))
    got[g] = send_ref[g]
    got_total[g] = total_ref[g]
    for copy in copies:
        copy.wait()
    before = [[None] * GROUP, [None] * GROUP]
    for way in range(2):
        order = range(GROUP) if way == 0 else range(GROUP - 1, -1, -1)
        carry = jnp.zeros(got.shape[2:], F32)
        passed = jnp.zeros(got_total.shape[2:], F32)
        for s in order:
            inner[s, way] = carry
            before[way][s] = jnp.exp(passed[:1])
            carry = jnp.exp(got_total[s, way][:1]) * carry + got[s, way].astype(F32)
            passed = passed + got_total[s, way]
        group[way] = carry.astype(BF16)
        group_total[way] = passed

    copies = []
    for d in range(1, outer):
        way = (z + d) // outer
        to = peer((z + d) % outer, g)
        copies.append(push(group_total.at[way], far_total.at[z], send2, recv2, 2 * d - 1, to))
        copies.append(push(group.at[way], far.at[z], send2, recv2, 2 * d - 2, to))
    far[z] = jnp.zeros(far.shape[1:], BF16)
    far_total[z] = jnp.zeros(far_total.shape[1:], F32)
    for copy in copies:
        copy.wait()
    for way in range(2):
        order = range(outer) if way == 0 else range(outer - 1, -1, -1)
        carry = jnp.zeros(far.shape[1:], F32)
        for s in order:
            longer = jnp.exp(far_total[s][:1]) * carry + far[s].astype(F32)
            carry = jnp.where(s < z if way == 0 else s > z, longer, carry)
        for s in range(GROUP):
            back[s, way] = (inner[s, way] + before[way][s] * carry).astype(BF16)

    copies = []
    for d in range(1, GROUP):
        to = (g + d) % GROUP
        copies.append(push(back.at[to], landed.at[g], send3, recv3, d - 1, peer(z, to)))
    landed[g] = back[g]
    for copy in copies:
        copy.wait()
    enter_ref[...] = landed[...]


def mix_kernel(proj_ref, both_ref, raw_ref, rate_ref, gain_ref, local_ref, enter_ref, out_ref, wide):
    heads2 = raw_ref.shape[1]
    heads = heads2 // 2
    width = heads * HEAD_DIM
    chunks = raw_ref.shape[0] // CHUNK
    quarter = width // GROUP
    for g in range(GROUP):
        for way in range(2):
            start = way * width + g * quarter
            wide[:, start : start + quarter] = enter_ref[g, way].astype(F32)
    spread = spread_matrix(heads2, BF16, 2)
    spread_one = spread_matrix(heads, BF16, 2)
    spread_wide = spread_matrix(heads2, F32)
    forward = lax.broadcasted_iota(jnp.int32, (CHUNK, heads2), 1) < heads
    rows_of = lax.broadcasted_iota(jnp.int32, (CHUNK, CHUNK), 0)
    cols_of = lax.broadcasted_iota(jnp.int32, (CHUNK, CHUNK), 1)
    lower = rows_of > cols_of
    on_line = rows_of == cols_of
    first_half = lax.broadcasted_iota(jnp.int32, (CHUNK, 2 * HEAD_DIM), 1) < HEAD_DIM
    decays = []
    for c in range(chunks):
        decays.append(chunk_decays(raw_ref[c * CHUNK : (c + 1) * CHUNK, :], rate_ref[...]))
    lasts = [upto[CHUNK - 1 : CHUNK, :] for _, upto, _ in decays]
    for c in range(chunks):
        rows = slice(c * CHUNK, (c + 1) * CHUNK)
        steps, upto, before = decays[c]
        last = lasts[c]
        column = jnp.where(forward, before, -upto)
        row = (jnp.where(forward, -upto, before) + jnp.log(steps)).T
        keys = both_ref[rows, :STATE]
        queries = both_ref[rows, STATE:]
        scores = dot(queries, keys, ((1,), (1,)))
        values = proj_ref[0, rows, :].astype(BF16)
        pieces = []
        for pair in range(heads // 2):
            weights = []
            for h in (2 * pair, 2 * pair + 1):
                power = jnp.where(
                    lower,
                    column[:, h : h + 1] + row[h : h + 1, :],
                    column[:, heads + h : heads + h + 1] + row[heads + h : heads + h + 1, :],
                )
                power = jnp.where(on_line, -jnp.inf, power)
                weights.append((scores * jnp.exp(power)).astype(BF16))
            both_values = values[:, pair * 2 * HEAD_DIM : (pair + 1) * 2 * HEAD_DIM]
            zero = jnp.zeros_like(both_values)
            stacked = jnp.concatenate(
                [
                    jnp.where(first_half, both_values, zero),
                    jnp.where(first_half, zero, both_values),
                ],
                axis=0,
            )
            pieces.append(dot(jnp.concatenate(weights, axis=1), stacked))
        mix = jnp.concatenate(pieces, axis=1)
        passed = jnp.zeros((1, heads2), F32)
        for other in range(chunks):
            if other < c:
                passed = passed + jnp.where(forward[:1], lasts[other], 0.0)
            if other > c:
                passed = passed + jnp.where(forward[:1], 0.0, lasts[other])
        passed = dot(jnp.broadcast_to(passed, (8, heads2)), spread_wide, precision=HIGH)[:1]
        entering = local_ref[c].astype(F32) + jnp.exp(passed) * wide[...]
        reach = dot(queries, entering.astype(BF16))
        scale = jnp.exp(jnp.where(forward, before, last - upto))
        reach = reach * dot(split_wide(scale), spread)
        mix = mix + reach[:, :width] + reach[:, width:]
        mix = mix + gain_ref[...] * values.astype(F32)
        gates = proj_ref[1, rows, :]
        gated = mix * (gates / (1.0 + jnp.exp(-gates)))
        square = gated * gated
        high = square.astype(BF16)
        low = (square - high.astype(F32)).astype(BF16)
        unit = spread_one[:heads]
        power = dot(high, unit, ((1,), (1,))) + dot(low, unit, ((1,), (1,)))
        norm = lax.rsqrt(power * (1.0 / HEAD_DIM) + 1e-05)
        out_ref[rows, :] = (gated * dot(split_wide(norm), spread_one)).astype(BF16)


def shards(tokens, in_weight, bc_weight, dt_weight, dt_bias, decay_rate, skip_gain, out_weight):
    heads = decay_rate.shape[0]
    width = heads * HEAD_DIM
    quarter = width // GROUP
    outer = lax.axis_size("seq") // GROUP
    whole = lax.all_gather(tokens, "tp", axis=1, tiled=True)
    length = whole.shape[0]
    chunks = length // CHUNK
    full_columns = lax.all_gather(bc_weight, "tp", axis=1, tiled=True)
    projected = jnp.einsum("td,dkf->ktf", whole, in_weight, preferred_element_type=F32)
    both = jnp.dot(whole, full_columns, preferred_element_type=F32).astype(BF16)
    raw = jnp.einsum("td,kdh->tkh", whole, dt_weight, preferred_element_type=F32)
    raw = (raw + dt_bias[None]).reshape(length, 2 * heads)
    rate = jnp.concatenate([decay_rate, decay_rate])[None, :]
    gain = jnp.repeat(skip_gain, HEAD_DIM)[None, :]
    params = pltpu.CompilerParams(vmem_limit_bytes=VMEM_LIMIT)
    vmem = pl.BlockSpec(memory_space=pltpu.VMEM)
    local, send, total = pl.pallas_call(
        states_kernel,
        out_shape=(
            jax.ShapeDtypeStruct((chunks, STATE, 2 * width), BF16),
            jax.ShapeDtypeStruct((GROUP, 2, STATE, quarter), BF16),
            jax.ShapeDtypeStruct((GROUP, 2, 8, quarter), F32),
        ),
        grid=(1,),
        in_specs=[
            pl.BlockSpec((1, length, width), lambda i: (0, 0, 0)),
            pl.BlockSpec((length, 2 * STATE), lambda i: (0, 0)),
            pl.BlockSpec((length, 2 * heads), lambda i: (0, 0)),
            pl.BlockSpec((1, 2 * heads), lambda i: (0, 0)),
        ],
        out_specs=(vmem, vmem, vmem),
        scratch_shapes=[pltpu.VMEM((chunks, STATE, 2 * width), F32)],
        compiler_params=params,
        name="block_states",
    )(projected, both, raw, rate)
    enter = pl.pallas_call(
        functools.partial(carry_kernel, outer),
        out_shape=jax.ShapeDtypeStruct((GROUP, 2, STATE, quarter), BF16),
        in_specs=[vmem, vmem],
        out_specs=vmem,
        scratch_shapes=[
            pltpu.VMEM((GROUP, 2, STATE, quarter), BF16),
            pltpu.VMEM((GROUP, 2, 8, quarter), F32),
            pltpu.VMEM((GROUP, 2, STATE, quarter), F32),
            pltpu.VMEM((2, STATE, quarter), BF16),
            pltpu.VMEM((2, 8, quarter), F32),
            pltpu.VMEM((outer, STATE, quarter), BF16),
            pltpu.VMEM((outer, 8, quarter), F32),
            pltpu.VMEM((GROUP, 2, STATE, quarter), BF16),
            pltpu.VMEM((GROUP, 2, STATE, quarter), BF16),
            pltpu.SemaphoreType.DMA((2 * GROUP - 2,)),
            pltpu.SemaphoreType.DMA((2 * GROUP - 2,)),
            pltpu.SemaphoreType.DMA((2 * outer - 2,)),
            pltpu.SemaphoreType.DMA((2 * outer - 2,)),
            pltpu.SemaphoreType.DMA((GROUP - 1,)),
            pltpu.SemaphoreType.DMA((GROUP - 1,)),
        ],
        compiler_params=pltpu.CompilerParams(
            vmem_limit_bytes=VMEM_LIMIT, collective_id=0, has_side_effects=True
        ),
        name="carry_states",
    )(send, total)
    hidden = pl.pallas_call(
        mix_kernel,
        out_shape=jax.ShapeDtypeStruct((length, width), BF16),
        in_specs=[vmem] * 7,
        out_specs=vmem,
        scratch_shapes=[pltpu.VMEM((STATE, 2 * width), F32)],
        compiler_params=params,
        name="mix_chunks",
    )(projected, both, raw, rate, gain, local, enter)
    partial_terms = jnp.dot(hidden, out_weight, preferred_element_type=F32)
    return lax.psum_scatter(partial_terms.astype(BF16), "tp", scatter_dimension=1, tiled=True)


def solution(mesh):
    in_specs = (
        P("seq", "tp"),
        P(None, None, "tp"),
        P(None, "tp"),
        P(None, None, "tp"),
        P(None, "tp"),
        P("tp"),
        P("tp"),
        P("tp", None),
    )
    out_specs = P("seq", "tp")
    return jax.shard_map(shards, mesh=mesh, in_specs=in_specs, out_specs=out_specs, check_vma=False)
```

```python
import functools

import jax
import jax.numpy as jnp
from jax import lax
from jax.experimental import pallas as pl
from jax.experimental.pallas import tpu as pltpu
from jax.sharding import PartitionSpec as P

HEAD_DIM = 64
STATE = 128
CHUNK = 128
GROUP = 4
PARTS = 4
VMEM_LIMIT = 48 * 1024 * 1024
F32 = jnp.float32
BF16 = jnp.bfloat16
HIGH = lax.Precision.HIGHEST


def dot(a, b, contract=((1,), (0,)), precision=None):
    return lax.dot_general(
        a, b, (contract, ((), ())), precision=precision, preferred_element_type=F32
    )


def split_wide(value):
    high = value.astype(BF16)
    return jnp.concatenate([high, (value - high.astype(F32)).astype(BF16)], axis=1)


def spread_matrix(count, dtype, copies=1):
    rows = lax.broadcasted_iota(jnp.int32, (copies * count, count * HEAD_DIM), 0)
    lanes = lax.broadcasted_iota(jnp.int32, (copies * count, count * HEAD_DIM), 1)
    return (lax.rem(rows, count) == lanes // HEAD_DIM).astype(dtype)


def chunk_decays(raw, rate):
    steps = jnp.maximum(raw, 0.0) + jnp.log1p(jnp.exp(-jnp.abs(raw)))
    logs = -rate * steps
    rows = lax.broadcasted_iota(jnp.int32, (CHUNK, CHUNK), 0)
    cols = lax.broadcasted_iota(jnp.int32, (CHUNK, CHUNK), 1)
    running = (rows >= cols).astype(F32)
    upto = dot(running, logs, precision=HIGH)
    return steps, upto, upto - logs


def gather_kernel(n, tokens_ref, bc_ref, dt_ref, bias_ref, whole_ref, both_ref, raw_ref, columns, *sems):
    send_bc, recv_bc, send_tok, recv_tok = sems
    me = lax.axis_index("tp")
    length, width = tokens_ref.shape

    barrier = pltpu.get_barrier_semaphore()
    for d in range(1, n):
        pl.semaphore_signal(
            barrier, inc=1, device_id={"tp": (me + d) % n}, device_id_type=pl.DeviceIdType.MESH
        )
    pl.semaphore_wait(barrier, n - 1)

    def features(owner):
        return pl.ds(pl.multiple_of(owner * width, width), width)

    weights, parts = [], []
    for d in range(1, n):
        to = {"tp": (me + d) % n}
        weights.append(
            pltpu.make_async_remote_copy(
                src_ref=bc_ref,
                dst_ref=columns.at[me],
                send_sem=send_bc.at[d - 1],
                recv_sem=recv_bc.at[d - 1],
                device_id=to,
                device_id_type=pl.DeviceIdType.MESH,
            )
        )
        parts.append(
            pltpu.make_async_remote_copy(
                src_ref=tokens_ref,
                dst_ref=whole_ref.at[:, features(me)],
                send_sem=send_tok.at[d - 1],
                recv_sem=recv_tok.at[d - 1],
                device_id=to,
                device_id_type=pl.DeviceIdType.MESH,
            )
        )
    for copy in weights + parts:
        copy.start()
    whole_ref[:, features(me)] = tokens_ref[...]
    columns[me] = bc_ref[...]
    for copy in weights:
        copy.wait()
    both = None
    raw = bias_ref[...]
    for d in range(n):
        if d:
            parts[d - 1].wait()
        here = features((me + n - d) % n)
        part = tokens_ref[...] if d == 0 else whole_ref[:, here]
        new = jnp.concatenate([dot(part, columns[s, here, :]) for s in range(n)], axis=1)
        both = new if both is None else both + new
        raw = raw + dot(part, dt_ref[:, here], ((1,), (1,)))
    both_ref[...] = both.astype(BF16)
    raw_ref[...] = raw


def states_kernel(proj_ref, both_ref, raw_ref, rate_ref, local_ref, send_ref, total_ref, sums):
    heads2 = raw_ref.shape[1]
    heads = heads2 // 2
    width = heads * HEAD_DIM
    chunks = raw_ref.shape[0] // CHUNK
    spread = spread_matrix(heads2, BF16, 2)
    spread_wide = spread_matrix(heads2, F32)
    forward = lax.broadcasted_iota(jnp.int32, (CHUNK, heads2), 1) < heads
    totals = []
    for c in range(chunks):
        rows = pl.ds(c * CHUNK, CHUNK)
        steps, upto, before = chunk_decays(raw_ref[rows, :], rate_ref[...])
        last = upto[CHUNK - 1 : CHUNK, :]
        weight = jnp.exp(jnp.where(forward, last - upto, before)) * steps
        weight = dot(split_wide(weight), spread)
        values = proj_ref[0, rows, :].astype(BF16).astype(F32)
        weighted = (jnp.concatenate([values, values], axis=1) * weight).astype(BF16)
        sums[c] = dot(both_ref[rows, :STATE], weighted, ((0,), (0,)))
        totals.append(dot(jnp.broadcast_to(last, (8, heads2)), spread_wide, precision=HIGH))
    block = functools.reduce(jnp.add, totals)
    quarter = width // GROUP
    for way in range(2):
        side = slice(way * width, (way + 1) * width)
        order = range(chunks) if way == 0 else range(chunks - 1, -1, -1)
        carry = jnp.zeros((STATE, width), F32)
        for c in order:
            local_ref[c, :, side] = carry.astype(BF16)
            carry = jnp.exp(totals[c][:1, side]) * carry + sums[c, :, side]
        for g in range(GROUP):
            part = slice(g * quarter, (g + 1) * quarter)
            send_ref[g, way] = carry[:, part].astype(BF16)
            total_ref[g, way] = block[:, side][:, part]


def carry_kernel(
    outer,
    send_ref,
    total_ref,
    enter_ref,
    got,
    got_total,
    inner,
    group,
    group_total,
    far,
    far_total,
    back,
    landed,
    send1,
    recv1,
    send2,
    recv2,
    send3,
    recv3,
):
    seq = lax.axis_index("seq")
    z, g = seq // GROUP, seq % GROUP

    def peer(zz, gg):
        return {"seq": zz * GROUP + gg}

    barrier = pltpu.get_barrier_semaphore()
    for d in range(1, GROUP):
        pl.semaphore_signal(
            barrier, inc=1, device_id=peer(z, (g + d) % GROUP), device_id_type=pl.DeviceIdType.MESH
        )
    for d in range(1, outer):
        pl.semaphore_signal(
            barrier, inc=1, device_id=peer((z + d) % outer, g), device_id_type=pl.DeviceIdType.MESH
        )
    pl.semaphore_wait(barrier, GROUP - 1 + outer - 1)

    def push(source, target, sends, recvs, slot, where):
        copy = pltpu.make_async_remote_copy(
            src_ref=source,
            dst_ref=target,
            send_sem=sends.at[slot],
            recv_sem=recvs.at[slot],
            device_id=where,
            device_id_type=pl.DeviceIdType.MESH,
        )
        copy.start()
        return copy

    bands = [pl.ds(p * (STATE // PARTS), STATE // PARTS) for p in range(PARTS)]

    first = [[] for _ in bands]
    for d in range(1, GROUP):
        to = (g + d) % GROUP
        first[0].append(push(total_ref.at[to], got_total.at[g], send1, recv1, d - 1, peer(z, to)))
    for p, band in enumerate(bands):
        for d in range(1, GROUP):
            to = (g + d) % GROUP
            slot = (p + 1) * (GROUP - 1) + d - 1
            source = send_ref.at[to, :, band, :]
            first[p].append(push(source, got.at[g, :, band, :], send1, recv1, slot, peer(z, to)))
    got[g] = send_ref[g]
    got_total[g] = total_ref[g]
    far[z] = jnp.zeros(far.shape[1:], BF16)
    far_total[z] = jnp.zeros(far_total.shape[1:], F32)
    before = [[None] * GROUP, [None] * GROUP]
    second = [[] for _ in bands]
    for p, band in enumerate(bands):
        for copy in first[p]:
            copy.wait()
        for way in range(2):
            order = range(GROUP) if way == 0 else range(GROUP - 1, -1, -1)
            carry = jnp.zeros((STATE // PARTS, got.shape[3]), F32)
            passed = jnp.zeros(got_total.shape[2:], F32)
            for s in order:
                inner[s, way, band, :] = carry
                before[way][s] = jnp.exp(passed[:1])
                carry = jnp.exp(got_total[s, way][:1]) * carry + got[s, way, band, :].astype(F32)
                passed = passed + got_total[s, way]
            group[way, band, :] = carry.astype(BF16)
            if p == 0:
                group_total[way] = passed

        for d in range(1, outer):
            way = (z + d) // outer
            to = peer((z + d) % outer, g)
            if p == 0:
                total = group_total.at[way]
                second[p].append(push(total, far_total.at[z], send2, recv2, d - 1, to))
            slot = (p + 1) * (outer - 1) + d - 1
            source = group.at[way, band, :]
            second[p].append(push(source, far.at[z, band, :], send2, recv2, slot, to))

    third = []
    for p, band in enumerate(bands):
        for copy in second[p]:
            copy.wait()
        for way in range(2):
            order = range(outer) if way == 0 else range(outer - 1, -1, -1)
            carry = jnp.zeros((STATE // PARTS, far.shape[2]), F32)
            for s in order:
                longer = jnp.exp(far_total[s][:1]) * carry + far[s, band, :].astype(F32)
                carry = jnp.where(s < z if way == 0 else s > z, longer, carry)
            for s in range(GROUP):
                entering = inner[s, way, band, :] + before[way][s] * carry
                back[s, way, band, :] = entering.astype(BF16)

        for d in range(1, GROUP):
            to = (g + d) % GROUP
            slot = p * (GROUP - 1) + d - 1
            source = back.at[to, :, band, :]
            third.append(push(source, landed.at[g, :, band, :], send3, recv3, slot, peer(z, to)))
    landed[g] = back[g]
    for copy in third:
        copy.wait()
    enter_ref[...] = landed[...]


def mix_kernel(
    n,
    proj_ref,
    both_ref,
    raw_ref,
    rate_ref,
    gain_ref,
    local_ref,
    enter_ref,
    weight_ref,
    out_ref,
    wide,
    hidden,
    own,
    leaving,
    arrived,
    send,
    recv,
):
    me = lax.axis_index("tp")
    columns = out_ref.shape[1]
    barrier = pltpu.get_barrier_semaphore()
    for d in range(1, n):
        pl.semaphore_signal(
            barrier, inc=1, device_id={"tp": (me + d) % n}, device_id_type=pl.DeviceIdType.MESH
        )
    pl.semaphore_wait(barrier, n - 1)
    copies = []
    heads2 = raw_ref.shape[1]
    heads = heads2 // 2
    width = heads * HEAD_DIM
    chunks = raw_ref.shape[0] // CHUNK
    quarter = width // GROUP
    for g in range(GROUP):
        for way in range(2):
            start = way * width + g * quarter
            wide[:, start : start + quarter] = enter_ref[g, way].astype(F32)
    spread = spread_matrix(heads2, BF16, 2)
    spread_one = spread_matrix(heads, BF16, 2)
    spread_wide = spread_matrix(heads2, F32)
    forward = lax.broadcasted_iota(jnp.int32, (CHUNK, heads2), 1) < heads
    rows_of = lax.broadcasted_iota(jnp.int32, (CHUNK, CHUNK), 0)
    cols_of = lax.broadcasted_iota(jnp.int32, (CHUNK, CHUNK), 1)
    lower = rows_of > cols_of
    on_line = rows_of == cols_of
    first_half = lax.broadcasted_iota(jnp.int32, (CHUNK, 2 * HEAD_DIM), 1) < HEAD_DIM
    decays = []
    for c in range(chunks):
        decays.append(chunk_decays(raw_ref[c * CHUNK : (c + 1) * CHUNK, :], rate_ref[...]))
    lasts = [upto[CHUNK - 1 : CHUNK, :] for _, upto, _ in decays]
    for c in range(chunks):
        rows = slice(c * CHUNK, (c + 1) * CHUNK)
        steps, upto, before = decays[c]
        last = lasts[c]
        column = jnp.where(forward, before, -upto)
        row = (jnp.where(forward, -upto, before) + jnp.log(steps)).T
        keys = both_ref[rows, :STATE]
        queries = both_ref[rows, STATE:]
        scores = dot(queries, keys, ((1,), (1,)))
        values = proj_ref[0, rows, :].astype(BF16)
        pieces = []
        for pair in range(heads // 2):
            weights = []
            for h in (2 * pair, 2 * pair + 1):
                power = jnp.where(
                    lower,
                    column[:, h : h + 1] + row[h : h + 1, :],
                    column[:, heads + h : heads + h + 1] + row[heads + h : heads + h + 1, :],
                )
                power = jnp.where(on_line, -jnp.inf, power)
                weights.append((scores * jnp.exp(power)).astype(BF16))
            both_values = values[:, pair * 2 * HEAD_DIM : (pair + 1) * 2 * HEAD_DIM]
            zero = jnp.zeros_like(both_values)
            stacked = jnp.concatenate(
                [
                    jnp.where(first_half, both_values, zero),
                    jnp.where(first_half, zero, both_values),
                ],
                axis=0,
            )
            pieces.append(dot(jnp.concatenate(weights, axis=1), stacked))
        mix = jnp.concatenate(pieces, axis=1)
        passed = jnp.zeros((1, heads2), F32)
        for other in range(chunks):
            if other < c:
                passed = passed + jnp.where(forward[:1], lasts[other], 0.0)
            if other > c:
                passed = passed + jnp.where(forward[:1], 0.0, lasts[other])
        passed = dot(jnp.broadcast_to(passed, (8, heads2)), spread_wide, precision=HIGH)[:1]
        entering = local_ref[c].astype(F32) + jnp.exp(passed) * wide[...]
        reach = dot(queries, entering.astype(BF16))
        scale = jnp.exp(jnp.where(forward, before, last - upto))
        reach = reach * dot(split_wide(scale), spread)
        mix = mix + reach[:, :width] + reach[:, width:]
        mix = mix + gain_ref[...] * values.astype(F32)
        gates = proj_ref[1, rows, :]
        gated = mix * (gates / (1.0 + jnp.exp(-gates)))
        square = gated * gated
        high = square.astype(BF16)
        low = (square - high.astype(F32)).astype(BF16)
        unit = spread_one[:heads]
        power = dot(high, unit, ((1,), (1,))) + dot(low, unit, ((1,), (1,)))
        norm = lax.rsqrt(power * (1.0 / HEAD_DIM) + 1e-05)
        hidden[rows, :] = (gated * dot(split_wide(norm), spread_one)).astype(BF16)
        if c % 2 == 0:
            continue
        rows = slice((c - 1) * CHUNK, (c + 1) * CHUNK)
        for d in range(1, n):
            to = (me + d) % n
            theirs = pl.ds(pl.multiple_of(to * columns, columns), columns)
            leaving[d - 1, rows, :] = dot(hidden[rows, :], weight_ref[:, theirs]).astype(BF16)
            slot = c // 2 * (n - 1) + d - 1
            copy = pltpu.make_async_remote_copy(
                src_ref=leaving.at[d - 1, rows, :],
                dst_ref=arrived.at[d - 1, rows, :],
                send_sem=send.at[slot],
                recv_sem=recv.at[slot],
                device_id={"tp": to},
                device_id_type=pl.DeviceIdType.MESH,
            )
            copy.start()
            copies.append(copy)
        mine = pl.ds(pl.multiple_of(me * columns, columns), columns)
        own[rows, :] = dot(hidden[rows, :], weight_ref[:, mine]).astype(BF16)
    for copy in copies:
        copy.wait()
    total = own[...].astype(F32)
    for d in range(1, n):
        total = total + arrived[d - 1].astype(F32)
    out_ref[...] = total.astype(BF16)


def shards(tokens, in_weight, bc_weight, dt_weight, dt_bias, decay_rate, skip_gain, out_weight):
    heads = decay_rate.shape[0]
    width = heads * HEAD_DIM
    quarter = width // GROUP
    outer = lax.axis_size("seq") // GROUP
    n = lax.axis_size("tp")
    length = tokens.shape[0]
    features = dt_weight.shape[1]
    chunks = length // CHUNK
    params = pltpu.CompilerParams(vmem_limit_bytes=VMEM_LIMIT)
    vmem = pl.BlockSpec(memory_space=pltpu.VMEM)
    whole, both, raw = pl.pallas_call(
        functools.partial(gather_kernel, n),
        out_shape=(
            jax.ShapeDtypeStruct((length, features), BF16),
            jax.ShapeDtypeStruct((length, 2 * STATE), BF16),
            jax.ShapeDtypeStruct((length, 2 * heads), F32),
        ),
        in_specs=[vmem] * 4,
        out_specs=(vmem, vmem, vmem),
        scratch_shapes=[pltpu.VMEM((n,) + bc_weight.shape, BF16)]
        + [pltpu.SemaphoreType.DMA((n - 1,))] * 4,
        compiler_params=pltpu.CompilerParams(
            vmem_limit_bytes=VMEM_LIMIT, collective_id=1, has_side_effects=True
        ),
        name="gather_features",
    )(
        tokens,
        bc_weight,
        dt_weight.transpose(0, 2, 1).reshape(2 * heads, features),
        dt_bias.reshape(1, 2 * heads),
    )
    projected = jnp.einsum("td,dkf->ktf", whole, in_weight, preferred_element_type=F32)
    rate = jnp.concatenate([decay_rate, decay_rate])[None, :]
    gain = jnp.repeat(skip_gain, HEAD_DIM)[None, :]
    local, send, total = pl.pallas_call(
        states_kernel,
        out_shape=(
            jax.ShapeDtypeStruct((chunks, STATE, 2 * width), BF16),
            jax.ShapeDtypeStruct((GROUP, 2, STATE, quarter), BF16),
            jax.ShapeDtypeStruct((GROUP, 2, 8, quarter), F32),
        ),
        grid=(1,),
        in_specs=[
            pl.BlockSpec((1, length, width), lambda i: (0, 0, 0)),
            pl.BlockSpec((length, 2 * STATE), lambda i: (0, 0)),
            pl.BlockSpec((length, 2 * heads), lambda i: (0, 0)),
            pl.BlockSpec((1, 2 * heads), lambda i: (0, 0)),
        ],
        out_specs=(vmem, vmem, vmem),
        scratch_shapes=[pltpu.VMEM((chunks, STATE, 2 * width), F32)],
        compiler_params=params,
        name="block_states",
    )(projected, both, raw, rate)
    enter = pl.pallas_call(
        functools.partial(carry_kernel, outer),
        out_shape=jax.ShapeDtypeStruct((GROUP, 2, STATE, quarter), BF16),
        in_specs=[vmem, vmem],
        out_specs=vmem,
        scratch_shapes=[
            pltpu.VMEM((GROUP, 2, STATE, quarter), BF16),
            pltpu.VMEM((GROUP, 2, 8, quarter), F32),
            pltpu.VMEM((GROUP, 2, STATE, quarter), F32),
            pltpu.VMEM((2, STATE, quarter), BF16),
            pltpu.VMEM((2, 8, quarter), F32),
            pltpu.VMEM((outer, STATE, quarter), BF16),
            pltpu.VMEM((outer, 8, quarter), F32),
            pltpu.VMEM((GROUP, 2, STATE, quarter), BF16),
            pltpu.VMEM((GROUP, 2, STATE, quarter), BF16),
            pltpu.SemaphoreType.DMA(((PARTS + 1) * (GROUP - 1),)),
            pltpu.SemaphoreType.DMA(((PARTS + 1) * (GROUP - 1),)),
            pltpu.SemaphoreType.DMA(((PARTS + 1) * (outer - 1),)),
            pltpu.SemaphoreType.DMA(((PARTS + 1) * (outer - 1),)),
            pltpu.SemaphoreType.DMA((PARTS * (GROUP - 1),)),
            pltpu.SemaphoreType.DMA((PARTS * (GROUP - 1),)),
        ],
        compiler_params=pltpu.CompilerParams(
            vmem_limit_bytes=VMEM_LIMIT, collective_id=0, has_side_effects=True
        ),
        name="carry_states",
    )(send, total)
    columns = out_weight.shape[1] // n
    return pl.pallas_call(
        functools.partial(mix_kernel, n),
        out_shape=jax.ShapeDtypeStruct((length, columns), BF16),
        in_specs=[vmem] * 8,
        out_specs=vmem,
        scratch_shapes=[
            pltpu.VMEM((STATE, 2 * width), F32),
            pltpu.VMEM((length, width), BF16),
            pltpu.VMEM((length, columns), BF16),
            pltpu.VMEM((n - 1, length, columns), BF16),
            pltpu.VMEM((n - 1, length, columns), BF16),
            pltpu.SemaphoreType.DMA((chunks // 2 * (n - 1),)),
            pltpu.SemaphoreType.DMA((chunks // 2 * (n - 1),)),
        ],
        compiler_params=pltpu.CompilerParams(
            vmem_limit_bytes=VMEM_LIMIT, collective_id=2, has_side_effects=True
        ),
        name="mix_chunks",
    )(projected, both, raw, rate, gain, local, enter, out_weight)


def solution(mesh):
    in_specs = (
        P("seq", "tp"),
        P(None, None, "tp"),
        P(None, "tp"),
        P(None, None, "tp"),
        P(None, "tp"),
        P("tp"),
        P("tp"),
        P("tp", None),
    )
    out_specs = P("seq", "tp")
    return jax.shard_map(shards, mesh=mesh, in_specs=in_specs, out_specs=out_specs, check_vma=False)
```

```python
import functools

import jax
import jax.numpy as jnp
from jax import lax
from jax.experimental import pallas as pl
from jax.experimental.pallas import tpu as pltpu
from jax.sharding import PartitionSpec as P

HEAD_DIM = 64
STATE = 128
CHUNK = 128
GROUP = 4
PARTS = 4
VMEM_LIMIT = 48 * 1024 * 1024
F32 = jnp.float32
BF16 = jnp.bfloat16
HIGH = lax.Precision.HIGHEST


def dot(a, b, contract=((1,), (0,)), precision=None):
    return lax.dot_general(
        a, b, (contract, ((), ())), precision=precision, preferred_element_type=F32
    )


def split_wide(value):
    high = value.astype(BF16)
    return jnp.concatenate([high, (value - high.astype(F32)).astype(BF16)], axis=1)


def spread_matrix(count, dtype, copies=1):
    rows = lax.broadcasted_iota(jnp.int32, (copies * count, count * HEAD_DIM), 0)
    lanes = lax.broadcasted_iota(jnp.int32, (copies * count, count * HEAD_DIM), 1)
    return (lax.rem(rows, count) == lanes // HEAD_DIM).astype(dtype)


def gather_kernel(n, tokens_ref, bc_ref, dt_ref, bias_ref, whole_ref, both_ref, raw_ref, *scratch):
    columns, dt, send_bc, recv_bc, send_tok, recv_tok, here_sem = scratch
    me = lax.axis_index("tp")
    width = tokens_ref.shape[1]

    def features(owner):
        return pl.ds(pl.multiple_of(owner * width, width), width)

    own_bc = pltpu.make_async_copy(bc_ref, columns.at[me], here_sem.at[0])
    own_tokens = pltpu.make_async_copy(tokens_ref, whole_ref.at[:, features(me)], here_sem.at[1])
    own_dt = pltpu.make_async_copy(dt_ref, dt, here_sem.at[2])
    barrier = pltpu.get_barrier_semaphore()
    for d in range(1, n):
        pl.semaphore_signal(
            barrier, inc=1, device_id={"tp": (me + d) % n}, device_id_type=pl.DeviceIdType.MESH
        )
    own_bc.start()
    own_tokens.start()
    own_dt.start()
    pl.semaphore_wait(barrier, n - 1)
    weights, parts = [], []
    for d in range(1, n):
        to = {"tp": (me + d) % n}
        weights.append(
            pltpu.make_async_remote_copy(
                src_ref=bc_ref,
                dst_ref=columns.at[me],
                send_sem=send_bc.at[d - 1],
                recv_sem=recv_bc.at[d - 1],
                device_id=to,
                device_id_type=pl.DeviceIdType.MESH,
            )
        )
        parts.append(
            pltpu.make_async_remote_copy(
                src_ref=tokens_ref,
                dst_ref=whole_ref.at[:, features(me)],
                send_sem=send_tok.at[d - 1],
                recv_sem=recv_tok.at[d - 1],
                device_id=to,
                device_id_type=pl.DeviceIdType.MESH,
            )
        )
    for copy in weights + parts:
        copy.start()
    own_bc.wait()
    own_tokens.wait()
    own_dt.wait()
    for copy in weights:
        copy.wait()
    both = None
    raw = jnp.concatenate([bias_ref[:1, :], bias_ref[1:, :]], axis=1)
    for d in range(n):
        if d:
            parts[d - 1].wait()
        here = features((me + n - d) % n)
        part = whole_ref[:, here]
        new = jnp.concatenate([dot(part, columns[s, here, :]) for s in range(n)], axis=1)
        both = new if both is None else both + new
        raw = raw + dot(part, dt[:, here], ((1,), (1,)))
    both_ref[...] = both.astype(BF16)
    raw_ref[...] = raw


def mixer_kernel(
    outer,
    n,
    proj_ref,
    both_ref,
    raw_ref,
    rate_ref,
    gain_ref,
    weight_hbm,
    out_ref,
    values_wide,
    gates,
    weight_ref,
    sums,
    local,
    mix,
    send_ref,
    total_ref,
    got,
    got_total,
    inner,
    group,
    group_total,
    far,
    far_total,
    back,
    landed,
    hidden,
    own,
    leaving,
    arrived,
    send1,
    recv1,
    send2,
    recv2,
    send3,
    recv3,
    send4,
    recv4,
    here_sem,
):
    seq = lax.axis_index("seq")
    me = lax.axis_index("tp")
    z, g = seq // GROUP, seq % GROUP
    heads2 = raw_ref.shape[1]
    heads = heads2 // 2
    width = heads * HEAD_DIM
    chunks = raw_ref.shape[0] // CHUNK
    quarter = width // GROUP
    columns = out_ref.shape[1]

    get_values = pltpu.make_async_copy(proj_ref.at[0], values_wide, here_sem.at[0])
    get_gates = pltpu.make_async_copy(proj_ref.at[1], gates, here_sem.at[1])
    get_weight = pltpu.make_async_copy(weight_hbm, weight_ref, here_sem.at[2])
    get_values.start()
    get_gates.start()
    get_weight.start()

    def peer(zz, gg):
        return {"seq": zz * GROUP + gg}

    barrier = pltpu.get_barrier_semaphore()
    friends = [peer(z, (g + d) % GROUP) for d in range(1, GROUP)]
    friends += [peer((z + d) % outer, g) for d in range(1, outer)]
    friends += [{"tp": (me + d) % n} for d in range(1, n)]
    for friend in friends:
        pl.semaphore_signal(barrier, inc=1, device_id=friend, device_id_type=pl.DeviceIdType.MESH)

    def push(source, target, sends, recvs, slot, where):
        copy = pltpu.make_async_remote_copy(
            src_ref=source,
            dst_ref=target,
            send_sem=sends.at[slot],
            recv_sem=recvs.at[slot],
            device_id=where,
            device_id_type=pl.DeviceIdType.MESH,
        )
        copy.start()
        return copy

    every = chunks * heads2
    raw = jnp.concatenate(
        [raw_ref[c * CHUNK : (c + 1) * CHUNK, :] for c in range(chunks)], axis=1
    )
    rate = jnp.concatenate([rate_ref[...]] * (2 * chunks), axis=1)
    steps = jnp.maximum(raw, 0.0) + jnp.log1p(jnp.exp(-jnp.abs(raw)))
    logs = -rate * steps
    rows_of = lax.broadcasted_iota(jnp.int32, (CHUNK, CHUNK), 0)
    cols_of = lax.broadcasted_iota(jnp.int32, (CHUNK, CHUNK), 1)
    upto = dot((rows_of >= cols_of).astype(F32), logs, precision=HIGH)
    before = upto - logs
    last = upto[CHUNK - 1 : CHUNK, :]
    forward = lax.rem(lax.broadcasted_iota(jnp.int32, (CHUNK, every), 1), heads2) < heads
    weight = jnp.exp(jnp.where(forward, last - upto, before)) * steps
    column = jnp.where(forward, before, -upto)
    row = (jnp.where(forward, -upto, before) + jnp.log(steps)).T
    scale = jnp.exp(jnp.where(forward, before, last - upto))
    lasts = [last[:, c * heads2 : (c + 1) * heads2] for c in range(chunks)]
    passed = []
    for c in range(chunks):
        gone = jnp.zeros((1, heads2), F32)
        for other in range(chunks):
            if other < c:
                gone = gone + jnp.where(forward[:1, :heads2], lasts[other], 0.0)
            if other > c:
                gone = gone + jnp.where(forward[:1, :heads2], 0.0, lasts[other])
        passed.append(gone)
    enter_scale = scale * jnp.exp(jnp.concatenate(passed, axis=1))
    spread = spread_matrix(heads2, BF16, 2)
    spread_one = spread_matrix(heads, BF16, 2)
    stack = lasts + [functools.reduce(jnp.add, lasts)]
    stack = stack + [jnp.zeros((1, heads2), F32)] * (8 - len(stack))
    totals = dot(jnp.concatenate(stack, axis=0), spread_matrix(heads2, F32), precision=HIGH)
    gain = jnp.broadcast_to(gain_ref[...], (8, heads))
    gain = dot(gain, spread_matrix(heads, F32), precision=HIGH)[:1]

    def spread_chunk(value, c):
        return dot(split_wide(value[:, c * heads2 : (c + 1) * heads2]), spread)

    get_values.wait()
    for c in range(chunks):
        rows = slice(c * CHUNK, (c + 1) * CHUNK)
        values = values_wide[rows, :].astype(BF16).astype(F32)
        weighted = jnp.concatenate([values, values], axis=1) * spread_chunk(weight, c)
        sums[c] = dot(both_ref[rows, :STATE], weighted.astype(BF16), ((0,), (0,)))
    for way in range(2):
        side = slice(way * width, (way + 1) * width)
        carry = jnp.zeros((STATE, width), F32)
        for c in range(chunks) if way == 0 else range(chunks - 1, -1, -1):
            local[c, :, side] = carry.astype(BF16)
            carry = jnp.exp(totals[c : c + 1, side]) * carry + sums[c, :, side]
        for q in range(GROUP):
            part = slice(q * quarter, (q + 1) * quarter)
            send_ref[q, way] = carry[:, part].astype(BF16)
            total = totals[chunks : chunks + 1, side][:, part]
            total_ref[q, way] = jnp.broadcast_to(total, (8, quarter))

    pl.semaphore_wait(barrier, GROUP - 1 + outer - 1 + n - 1)

    bands = [pl.ds(p * (STATE // PARTS), STATE // PARTS) for p in range(PARTS)]

    first = [[] for _ in bands]
    for d in range(1, GROUP):
        to = (g + d) % GROUP
        first[0].append(push(total_ref.at[to], got_total.at[g], send1, recv1, d - 1, peer(z, to)))
    for p, band in enumerate(bands):
        for d in range(1, GROUP):
            to = (g + d) % GROUP
            slot = (p + 1) * (GROUP - 1) + d - 1
            source = send_ref.at[to, :, band, :]
            first[p].append(push(source, got.at[g, :, band, :], send1, recv1, slot, peer(z, to)))
    got[g] = send_ref[g]
    got_total[g] = total_ref[g]
    far[z] = jnp.zeros(far.shape[1:], BF16)
    far_total[z] = jnp.zeros(far_total.shape[1:], F32)

    lower = rows_of > cols_of
    on_line = rows_of == cols_of
    first_half = lax.broadcasted_iota(jnp.int32, (CHUNK, 2 * HEAD_DIM), 1) < HEAD_DIM

    def inside(c):
        rows = slice(c * CHUNK, (c + 1) * CHUNK)
        scores = dot(both_ref[rows, STATE:], both_ref[rows, :STATE], ((1,), (1,)))
        for pair in range(heads // 2):
            weights = []
            for h in (2 * pair, 2 * pair + 1):
                f = c * heads2 + h
                b = f + heads
                power = jnp.where(
                    lower,
                    column[:, f : f + 1] + row[f : f + 1, :],
                    column[:, b : b + 1] + row[b : b + 1, :],
                )
                power = jnp.where(on_line, -jnp.inf, power)
                weights.append((scores * jnp.exp(power)).astype(BF16))
            lanes = slice(pair * 2 * HEAD_DIM, (pair + 1) * 2 * HEAD_DIM)
            pair_values = values_wide[rows, lanes].astype(BF16)
            zero = jnp.zeros_like(pair_values)
            stacked = jnp.concatenate(
                [
                    jnp.where(first_half, pair_values, zero),
                    jnp.where(first_half, zero, pair_values),
                ],
                axis=0,
            )
            mix[rows, lanes] = dot(jnp.concatenate(weights, axis=1), stacked)

    def nearby(c):
        rows = slice(c * CHUNK, (c + 1) * CHUNK)
        reach = dot(both_ref[rows, STATE:], local[c]) * spread_chunk(scale, c)
        values = values_wide[rows, :].astype(BF16).astype(F32)
        mix[rows, :] = mix[rows, :] + reach[:, :width] + reach[:, width:] + gain * values

    inside(0)
    if chunks > 1:
        inside(1)
    before_state = [[None] * GROUP, [None] * GROUP]
    second = [[] for _ in bands]
    for p, band in enumerate(bands):
        for copy in first[p]:
            copy.wait()
        for way in range(2):
            carry = jnp.zeros((STATE // PARTS, quarter), F32)
            gone = jnp.zeros((8, quarter), F32)
            for s in range(GROUP) if way == 0 else range(GROUP - 1, -1, -1):
                inner[s, way, band, :] = carry
                before_state[way][s] = jnp.exp(gone[:1])
                carry = jnp.exp(got_total[s, way][:1]) * carry + got[s, way, band, :].astype(F32)
                gone = gone + got_total[s, way]
            group[way, band, :] = carry.astype(BF16)
            if p == 0:
                group_total[way] = gone

        for d in range(1, outer):
            way = (z + d) // outer
            to = peer((z + d) % outer, g)
            if p == 0:
                total = group_total.at[way]
                second[p].append(push(total, far_total.at[z], send2, recv2, d - 1, to))
            slot = (p + 1) * (outer - 1) + d - 1
            source = group.at[way, band, :]
            second[p].append(push(source, far.at[z, band, :], send2, recv2, slot, to))

    for c in range(2, chunks):
        inside(c)
    third = []
    for p, band in enumerate(bands):
        for copy in second[p]:
            copy.wait()
        for way in range(2):
            carry = jnp.zeros((STATE // PARTS, quarter), F32)
            for s in range(outer) if way == 0 else range(outer - 1, -1, -1):
                longer = jnp.exp(far_total[s][:1]) * carry + far[s, band, :].astype(F32)
                carry = jnp.where(s < z if way == 0 else s > z, longer, carry)
            for s in range(GROUP):
                entering = inner[s, way, band, :] + before_state[way][s] * carry
                back[s, way, band, :] = entering.astype(BF16)

        for d in range(1, GROUP):
            to = (g + d) % GROUP
            slot = p * (GROUP - 1) + d - 1
            source = back.at[to, :, band, :]
            third.append(push(source, landed.at[g, :, band, :], send3, recv3, slot, peer(z, to)))
    landed[g] = back[g]
    get_gates.wait()
    for c in range(chunks):
        nearby(c)
        rows = slice(c * CHUNK, (c + 1) * CHUNK)
        gates[rows, :] = gates[rows, :] / (1.0 + jnp.exp(-gates[rows, :]))
    get_weight.wait()
    for copy in third:
        copy.wait()

    copies = []
    for c in range(chunks):
        rows = slice(c * CHUNK, (c + 1) * CHUNK)
        queries = both_ref[rows, STATE:]
        reach = [dot(queries, landed[q, way]) for way in range(2) for q in range(GROUP)]
        reach = jnp.concatenate(reach, axis=1) * spread_chunk(enter_scale, c)
        gated = (mix[rows, :] + reach[:, :width] + reach[:, width:]) * gates[rows, :]
        square = gated * gated
        high = square.astype(BF16)
        low = (square - high.astype(F32)).astype(BF16)
        unit = spread_one[:heads]
        power = dot(high, unit, ((1,), (1,))) + dot(low, unit, ((1,), (1,)))
        norm = lax.rsqrt(power * (1.0 / HEAD_DIM) + 1e-05)
        hidden[rows, :] = (gated * dot(split_wide(norm), spread_one)).astype(BF16)
        if c % 2 == 0:
            continue
        rows = slice((c - 1) * CHUNK, (c + 1) * CHUNK)
        for d in range(1, n):
            to = (me + d) % n
            theirs = pl.ds(pl.multiple_of(to * columns, columns), columns)
            leaving[d - 1, rows, :] = dot(hidden[rows, :], weight_ref[:, theirs]).astype(BF16)
            slot = c // 2 * (n - 1) + d - 1
            source = leaving.at[d - 1, rows, :]
            copies.append(
                push(source, arrived.at[d - 1, rows, :], send4, recv4, slot, {"tp": to})
            )
        mine = pl.ds(pl.multiple_of(me * columns, columns), columns)
        own[rows, :] = dot(hidden[rows, :], weight_ref[:, mine]).astype(BF16)
    for copy in copies:
        copy.wait()
    total = own[...].astype(F32)
    for d in range(1, n):
        total = total + arrived[d - 1].astype(F32)
    out_ref[...] = total.astype(BF16)


def shards(tokens, in_weight, bc_weight, dt_weight, dt_bias, decay_rate, skip_gain, out_weight):
    heads = decay_rate.shape[0]
    width = heads * HEAD_DIM
    quarter = width // GROUP
    outer = lax.axis_size("seq") // GROUP
    n = lax.axis_size("tp")
    length = tokens.shape[0]
    features = dt_weight.shape[1]
    chunks = length // CHUNK
    columns = out_weight.shape[1] // n
    vmem = pl.BlockSpec(memory_space=pltpu.VMEM)
    anywhere = pl.BlockSpec(memory_space=pl.ANY)
    dma = pltpu.SemaphoreType.DMA
    whole, both, raw = pl.pallas_call(
        functools.partial(gather_kernel, n),
        out_shape=(
            jax.ShapeDtypeStruct((length, features), BF16),
            jax.ShapeDtypeStruct((length, 2 * STATE), BF16),
            jax.ShapeDtypeStruct((length, 2 * heads), F32),
        ),
        in_specs=[pl.BlockSpec(memory_space=pltpu.HBM)] * 3 + [vmem],
        out_specs=(vmem, vmem, vmem),
        scratch_shapes=[
            pltpu.VMEM((n,) + bc_weight.shape, BF16),
            pltpu.VMEM((2 * heads, features), BF16),
        ]
        + [dma((n - 1,))] * 4
        + [dma((3,))],
        compiler_params=pltpu.CompilerParams(
            vmem_limit_bytes=VMEM_LIMIT, collective_id=0, has_side_effects=True
        ),
        name="gather_features",
    )(
        tokens,
        bc_weight,
        dt_weight.transpose(0, 2, 1).reshape(2 * heads, features),
        dt_bias,
    )
    projected = jnp.einsum("td,dkf->ktf", whole, in_weight, preferred_element_type=F32)
    return pl.pallas_call(
        functools.partial(mixer_kernel, outer, n),
        out_shape=jax.ShapeDtypeStruct((length, columns), BF16),
        in_specs=[anywhere, vmem, vmem, vmem, vmem, anywhere],
        out_specs=vmem,
        scratch_shapes=[
            pltpu.VMEM((length, width), F32),
            pltpu.VMEM((length, width), F32),
            pltpu.VMEM(out_weight.shape, BF16),
            pltpu.VMEM((chunks, STATE, 2 * width), F32),
            pltpu.VMEM((chunks, STATE, 2 * width), BF16),
            pltpu.VMEM((length, width), F32),
            pltpu.VMEM((GROUP, 2, STATE, quarter), BF16),
            pltpu.VMEM((GROUP, 2, 8, quarter), F32),
            pltpu.VMEM((GROUP, 2, STATE, quarter), BF16),
            pltpu.VMEM((GROUP, 2, 8, quarter), F32),
            pltpu.VMEM((GROUP, 2, STATE, quarter), F32),
            pltpu.VMEM((2, STATE, quarter), BF16),
            pltpu.VMEM((2, 8, quarter), F32),
            pltpu.VMEM((outer, STATE, quarter), BF16),
            pltpu.VMEM((outer, 8, quarter), F32),
            pltpu.VMEM((GROUP, 2, STATE, quarter), BF16),
            pltpu.VMEM((GROUP, 2, STATE, quarter), BF16),
            pltpu.VMEM((length, width), BF16),
            pltpu.VMEM((length, columns), BF16),
            pltpu.VMEM((n - 1, length, columns), BF16),
            pltpu.VMEM((n - 1, length, columns), BF16),
        ]
        + [dma(((PARTS + 1) * (GROUP - 1),))] * 2
        + [dma(((PARTS + 1) * (outer - 1),))] * 2
        + [dma((PARTS * (GROUP - 1),))] * 2
        + [dma((chunks // 2 * (n - 1),))] * 2
        + [dma((3,))],
        compiler_params=pltpu.CompilerParams(
            vmem_limit_bytes=VMEM_LIMIT, collective_id=1, has_side_effects=True
        ),
        name="mixer",
    )(projected, both, raw, decay_rate[None], skip_gain[None], out_weight)


def solution(mesh):
    in_specs = (
        P("seq", "tp"),
        P(None, None, "tp"),
        P(None, "tp"),
        P(None, None, "tp"),
        P(None, "tp"),
        P("tp"),
        P("tp"),
        P("tp", None),
    )
    out_specs = P("seq", "tp")
    return jax.shard_map(shards, mesh=mesh, in_specs=in_specs, out_specs=out_specs, check_vma=False)
```

```python
import functools

import jax
import jax.numpy as jnp
from jax import lax
from jax.experimental import pallas as pl
from jax.experimental.pallas import tpu as pltpu
from jax.sharding import PartitionSpec as P

HEAD_DIM = 64
STATE = 128
CHUNK = 128
GROUP = 4
PARTS = 4
VMEM_LIMIT = 40 * 1024 * 1024
GATHER_LIMIT = 60 * 1024 * 1024
F32 = jnp.float32
BF16 = jnp.bfloat16
HIGH = lax.Precision.HIGHEST


def dot(a, b, contract=((1,), (0,)), precision=None):
    return lax.dot_general(
        a, b, (contract, ((), ())), precision=precision, preferred_element_type=F32
    )


def split_wide(value):
    high = value.astype(BF16)
    return jnp.concatenate([high, (value - high.astype(F32)).astype(BF16)], axis=1)


def spread_matrix(count, dtype, copies=1):
    rows = lax.broadcasted_iota(jnp.int32, (copies * count, count * HEAD_DIM), 0)
    lanes = lax.broadcasted_iota(jnp.int32, (copies * count, count * HEAD_DIM), 1)
    return (lax.rem(rows, count) == lanes // HEAD_DIM).astype(dtype)


def gather_kernel(n, tokens_ref, bc_ref, dt_ref, bias_ref, whole_ref, both_ref, raw_ref, *scratch):
    columns, dt, send_bc, recv_bc, send_tok, recv_tok, here_sem = scratch
    me = lax.axis_index("tp")
    width = tokens_ref.shape[1]

    def features(owner):
        return pl.ds(pl.multiple_of(owner * width, width), width)

    own_bc = pltpu.make_async_copy(bc_ref, columns.at[me], here_sem.at[0])
    own_tokens = pltpu.make_async_copy(tokens_ref, whole_ref.at[:, features(me)], here_sem.at[1])
    own_dt = pltpu.make_async_copy(dt_ref, dt, here_sem.at[2])
    barrier = pltpu.get_barrier_semaphore()
    for d in range(1, n):
        pl.semaphore_signal(
            barrier, inc=1, device_id={"tp": (me + d) % n}, device_id_type=pl.DeviceIdType.MESH
        )
    own_bc.start()
    own_tokens.start()
    own_dt.start()
    pl.semaphore_wait(barrier, n - 1)
    weights, parts = [], []
    for d in range(1, n):
        to = {"tp": (me + d) % n}
        weights.append(
            pltpu.make_async_remote_copy(
                src_ref=bc_ref,
                dst_ref=columns.at[me],
                send_sem=send_bc.at[d - 1],
                recv_sem=recv_bc.at[d - 1],
                device_id=to,
                device_id_type=pl.DeviceIdType.MESH,
            )
        )
        parts.append(
            pltpu.make_async_remote_copy(
                src_ref=tokens_ref,
                dst_ref=whole_ref.at[:, features(me)],
                send_sem=send_tok.at[d - 1],
                recv_sem=recv_tok.at[d - 1],
                device_id=to,
                device_id_type=pl.DeviceIdType.MESH,
            )
        )
    for copy in weights + parts:
        copy.start()
    own_bc.wait()
    own_tokens.wait()
    own_dt.wait()
    for copy in weights:
        copy.wait()
    both = None
    raw = jnp.concatenate([bias_ref[:1, :], bias_ref[1:, :]], axis=1)
    for d in range(n):
        if d:
            parts[d - 1].wait()
        here = features((me + n - d) % n)
        part = whole_ref[:, here]
        new = jnp.concatenate([dot(part, columns[s, here, :]) for s in range(n)], axis=1)
        both = new if both is None else both + new
        raw = raw + dot(part, dt[:, here], ((1,), (1,)))
    both_ref[...] = both.astype(BF16)
    raw_ref[...] = raw


def mixer_kernel(
    outer,
    n,
    proj_ref,
    both_ref,
    raw_ref,
    rate_ref,
    gain_ref,
    weight_hbm,
    own,
    arrived,
    values_wide,
    gates,
    weight_ref,
    weighted,
    turned,
    local,
    mix,
    send_ref,
    total_ref,
    got,
    got_total,
    inner,
    group,
    group_total,
    far,
    far_total,
    back,
    landed,
    hidden,
    leaving,
    send1,
    recv1,
    send2,
    recv2,
    send3,
    recv3,
    send4,
    recv4,
    here_sem,
):
    seq = lax.axis_index("seq")
    me = lax.axis_index("tp")
    z, g = seq // GROUP, seq % GROUP
    heads2 = raw_ref.shape[1]
    heads = heads2 // 2
    width = heads * HEAD_DIM
    chunks = raw_ref.shape[0] // CHUNK
    quarter = width // GROUP
    columns = own.shape[1]

    get_values = pltpu.make_async_copy(proj_ref.at[0], values_wide, here_sem.at[0])
    get_gates = pltpu.make_async_copy(proj_ref.at[1], gates, here_sem.at[1])
    get_weight = pltpu.make_async_copy(weight_hbm, weight_ref, here_sem.at[2])
    get_values.start()
    get_gates.start()
    get_weight.start()

    def peer(zz, gg):
        return {"seq": zz * GROUP + gg}

    barrier = pltpu.get_barrier_semaphore()
    friends = [peer(z, (g + d) % GROUP) for d in range(1, GROUP)]
    friends += [peer((z + d) % outer, g) for d in range(1, outer)]
    friends += [{"tp": (me + d) % n} for d in range(1, n)]
    for friend in friends:
        pl.semaphore_signal(barrier, inc=1, device_id=friend, device_id_type=pl.DeviceIdType.MESH)

    def push(source, target, sends, recvs, slot, where):
        copy = pltpu.make_async_remote_copy(
            src_ref=source,
            dst_ref=target,
            send_sem=sends.at[slot],
            recv_sem=recvs.at[slot],
            device_id=where,
            device_id_type=pl.DeviceIdType.MESH,
        )
        copy.start()
        return copy

    every = chunks * heads2
    raw = jnp.concatenate(
        [raw_ref[c * CHUNK : (c + 1) * CHUNK, :] for c in range(chunks)], axis=1
    )
    rate = jnp.concatenate([rate_ref[...]] * (2 * chunks), axis=1)
    steps = jnp.maximum(raw, 0.0) + jnp.log1p(jnp.exp(-jnp.abs(raw)))
    logs = -rate * steps
    rows_of = lax.broadcasted_iota(jnp.int32, (CHUNK, CHUNK), 0)
    cols_of = lax.broadcasted_iota(jnp.int32, (CHUNK, CHUNK), 1)
    upto = dot((rows_of >= cols_of).astype(F32), logs, precision=HIGH)
    before = upto - logs
    last = upto[CHUNK - 1 : CHUNK, :]
    forward = lax.rem(lax.broadcasted_iota(jnp.int32, (CHUNK, every), 1), heads2) < heads
    weight = jnp.exp(jnp.where(forward, last - upto, before)) * steps
    column = jnp.where(forward, before, -upto)
    row = (jnp.where(forward, -upto, before) + jnp.log(steps)).T
    scale = jnp.exp(jnp.where(forward, before, last - upto))
    lasts = [last[:, c * heads2 : (c + 1) * heads2] for c in range(chunks)]
    passed = []
    for c in range(chunks):
        gone = jnp.zeros((1, heads2), F32)
        for other in range(chunks):
            if other < c:
                gone = gone + jnp.where(forward[:1, :heads2], lasts[other], 0.0)
            if other > c:
                gone = gone + jnp.where(forward[:1, :heads2], 0.0, lasts[other])
        passed.append(gone)
    enter_scale = scale * jnp.exp(jnp.concatenate(passed, axis=1))
    spread = spread_matrix(heads2, BF16, 2)
    spread_one = spread_matrix(heads, BF16, 2)
    stack = lasts + [functools.reduce(jnp.add, lasts)]
    stack = stack + [jnp.zeros((1, heads2), F32)] * (8 - len(stack))
    totals = dot(jnp.concatenate(stack, axis=0), spread_matrix(heads2, F32), precision=HIGH)
    gain = jnp.broadcast_to(gain_ref[...], (8, heads))
    gain = dot(gain, spread_matrix(heads, F32), precision=HIGH)[:1]

    def spread_chunk(value, c):
        return dot(split_wide(value[:, c * heads2 : (c + 1) * heads2]), spread)

    get_values.wait()
    for c in range(chunks):
        rows = slice(c * CHUNK, (c + 1) * CHUNK)
        values = values_wide[rows, :].astype(BF16).astype(F32)
        wide = jnp.concatenate([values, values], axis=1) * spread_chunk(weight, c)
        weighted[c] = wide.astype(BF16)
        turned[c] = both_ref[rows, :STATE].T

    def block_state(rows):
        for way in range(2):
            side = slice(way * width, (way + 1) * width)
            carry = jnp.zeros((rows.stop - rows.start, width), F32)
            for c in range(chunks) if way == 0 else range(chunks - 1, -1, -1):
                local[c, rows, side] = carry.astype(BF16)
                new = dot(turned[c, rows, :], weighted[c, :, side])
                carry = jnp.exp(totals[c : c + 1, side]) * carry + new
            for q in range(GROUP):
                part = slice(q * quarter, (q + 1) * quarter)
                send_ref[q, way, rows, :] = carry[:, part].astype(BF16)

    for way in range(2):
        for q in range(GROUP):
            part = slice(way * width + q * quarter, way * width + (q + 1) * quarter)
            total_ref[q, way] = jnp.broadcast_to(totals[chunks : chunks + 1, part], (8, quarter))

    bands = [pl.ds(p * (STATE // PARTS), STATE // PARTS) for p in range(PARTS)]
    first = [[] for _ in bands]
    second = [[] for _ in bands]
    third = []
    before_state = [[None] * GROUP, [None] * GROUP]

    def share(p):
        for d in range(1, GROUP):
            to = (g + d) % GROUP
            if p == 0:
                total = total_ref.at[to]
                first[p].append(push(total, got_total.at[g], send1, recv1, d - 1, peer(z, to)))
            slot = (p + 1) * (GROUP - 1) + d - 1
            source = send_ref.at[to, :, bands[p], :]
            target = got.at[g, :, bands[p], :]
            first[p].append(push(source, target, send1, recv1, slot, peer(z, to)))

    def along(p):
        band = bands[p]
        for copy in first[p]:
            copy.wait()
        for way in range(2):
            carry = jnp.zeros((STATE // PARTS, quarter), F32)
            gone = jnp.zeros((8, quarter), F32)
            for s in range(GROUP) if way == 0 else range(GROUP - 1, -1, -1):
                inner[s, way, band, :] = carry
                before_state[way][s] = jnp.exp(gone[:1])
                carry = jnp.exp(got_total[s, way][:1]) * carry + got[s, way, band, :].astype(F32)
                gone = gone + got_total[s, way]
            group[way, band, :] = carry.astype(BF16)
            if p == 0:
                group_total[way] = gone
        for d in range(1, outer):
            way = (z + d) // outer
            to = peer((z + d) % outer, g)
            if p == 0:
                total = group_total.at[way]
                second[p].append(push(total, far_total.at[z], send2, recv2, d - 1, to))
            slot = (p + 1) * (outer - 1) + d - 1
            source = group.at[way, band, :]
            second[p].append(push(source, far.at[z, band, :], send2, recv2, slot, to))

    def hand_back(p):
        band = bands[p]
        for copy in second[p]:
            copy.wait()
        for way in range(2):
            carry = jnp.zeros((STATE // PARTS, quarter), F32)
            for s in range(outer) if way == 0 else range(outer - 1, -1, -1):
                longer = jnp.exp(far_total[s][:1]) * carry + far[s, band, :].astype(F32)
                carry = jnp.where(s < z if way == 0 else s > z, longer, carry)
            for s in range(GROUP):
                entering = inner[s, way, band, :] + before_state[way][s] * carry
                back[s, way, band, :] = entering.astype(BF16)
        for d in range(1, GROUP):
            to = (g + d) % GROUP
            slot = p * (GROUP - 1) + d - 1
            source = back.at[to, :, band, :]
            third.append(push(source, landed.at[g, :, band, :], send3, recv3, slot, peer(z, to)))

    half = STATE // 2
    block_state(slice(0, half))
    pl.semaphore_wait(barrier, GROUP - 1 + outer - 1 + n - 1)
    share(0)
    share(1)
    block_state(slice(half, STATE))
    got[g] = send_ref[g]
    got_total[g] = total_ref[g]
    far[z] = jnp.zeros(far.shape[1:], BF16)
    far_total[z] = jnp.zeros(far_total.shape[1:], F32)

    lower = rows_of > cols_of
    on_line = rows_of == cols_of
    first_half = lax.broadcasted_iota(jnp.int32, (CHUNK, 2 * HEAD_DIM), 1) < HEAD_DIM

    def inside(c):
        rows = slice(c * CHUNK, (c + 1) * CHUNK)
        scores = dot(both_ref[rows, STATE:], both_ref[rows, :STATE], ((1,), (1,)))
        for pair in range(heads // 2):
            weights = []
            for h in (2 * pair, 2 * pair + 1):
                f = c * heads2 + h
                b = f + heads
                power = jnp.where(
                    lower,
                    column[:, f : f + 1] + row[f : f + 1, :],
                    column[:, b : b + 1] + row[b : b + 1, :],
                )
                power = jnp.where(on_line, -jnp.inf, power)
                weights.append((scores * jnp.exp(power)).astype(BF16))
            lanes = slice(pair * 2 * HEAD_DIM, (pair + 1) * 2 * HEAD_DIM)
            pair_values = values_wide[rows, lanes].astype(BF16)
            zero = jnp.zeros_like(pair_values)
            stacked = jnp.concatenate(
                [
                    jnp.where(first_half, pair_values, zero),
                    jnp.where(first_half, zero, pair_values),
                ],
                axis=0,
            )
            mix[rows, lanes] = dot(jnp.concatenate(weights, axis=1), stacked)

    def nearby(c):
        rows = slice(c * CHUNK, (c + 1) * CHUNK)
        reach = dot(both_ref[rows, STATE:], local[c]) * spread_chunk(scale, c)
        values = values_wide[rows, :].astype(BF16).astype(F32)
        mix[rows, :] = mix[rows, :] + reach[:, :width] + reach[:, width:] + gain * values

    def activate(c):
        rows = slice(c * CHUNK, (c + 1) * CHUNK)
        gates[rows, :] = gates[rows, :] / (1.0 + jnp.exp(-gates[rows, :]))

    inside(0)
    along(0)
    share(2)
    inside(1)
    along(1)
    share(3)
    inside(2)
    along(2)
    hand_back(0)
    inside(3)
    along(3)
    hand_back(1)
    nearby(0)
    nearby(1)
    hand_back(2)
    nearby(2)
    nearby(3)
    hand_back(3)
    landed[g] = back[g]
    get_gates.wait()
    for c in range(chunks):
        activate(c)
    get_weight.wait()
    for copy in third:
        copy.wait()

    copies = []
    for c in range(chunks):
        rows = slice(c * CHUNK, (c + 1) * CHUNK)
        queries = both_ref[rows, STATE:]
        reach = [dot(queries, landed[q, way]) for way in range(2) for q in range(GROUP)]
        reach = jnp.concatenate(reach, axis=1) * spread_chunk(enter_scale, c)
        gated = (mix[rows, :] + reach[:, :width] + reach[:, width:]) * gates[rows, :]
        square = gated * gated
        high = square.astype(BF16)
        low = (square - high.astype(F32)).astype(BF16)
        unit = spread_one[:heads]
        power = dot(high, unit, ((1,), (1,))) + dot(low, unit, ((1,), (1,)))
        norm = lax.rsqrt(power * (1.0 / HEAD_DIM) + 1e-05)
        hidden[rows, :] = (gated * dot(split_wide(norm), spread_one)).astype(BF16)
        if c % 2 == 0:
            continue
        rows = slice((c - 1) * CHUNK, (c + 1) * CHUNK)
        for d in range(1, n):
            to = (me + d) % n
            theirs = pl.ds(pl.multiple_of(to * columns, columns), columns)
            leaving[d - 1, rows, :] = dot(hidden[rows, :], weight_ref[:, theirs]).astype(BF16)
            slot = c // 2 * (n - 1) + d - 1
            source = leaving.at[d - 1, rows, :]
            copies.append(
                push(source, arrived.at[d - 1, rows, :], send4, recv4, slot, {"tp": to})
            )
    mine = pl.ds(pl.multiple_of(me * columns, columns), columns)
    own[...] = dot(hidden[...], weight_ref[:, mine]).astype(BF16)
    for copy in copies:
        copy.wait()


def shards(tokens, in_weight, bc_weight, dt_weight, dt_bias, decay_rate, skip_gain, out_weight):
    heads = decay_rate.shape[0]
    width = heads * HEAD_DIM
    quarter = width // GROUP
    outer = lax.axis_size("seq") // GROUP
    n = lax.axis_size("tp")
    length = tokens.shape[0]
    features = dt_weight.shape[1]
    chunks = length // CHUNK
    columns = out_weight.shape[1] // n
    vmem = pl.BlockSpec(memory_space=pltpu.VMEM)
    anywhere = pl.BlockSpec(memory_space=pl.ANY)
    dma = pltpu.SemaphoreType.DMA
    whole, both, raw = pl.pallas_call(
        functools.partial(gather_kernel, n),
        out_shape=(
            jax.ShapeDtypeStruct((length, features), BF16),
            jax.ShapeDtypeStruct((length, 2 * STATE), BF16),
            jax.ShapeDtypeStruct((length, 2 * heads), F32),
        ),
        in_specs=[pl.BlockSpec(memory_space=pltpu.HBM)] * 3 + [vmem],
        out_specs=(vmem, vmem, vmem),
        scratch_shapes=[
            pltpu.VMEM((n,) + bc_weight.shape, BF16),
            pltpu.VMEM((2 * heads, features), BF16),
        ]
        + [dma((n - 1,))] * 4
        + [dma((3,))],
        compiler_params=pltpu.CompilerParams(
            vmem_limit_bytes=GATHER_LIMIT, collective_id=0, has_side_effects=True
        ),
        name="gather_features",
    )(
        tokens,
        bc_weight,
        dt_weight.transpose(0, 2, 1).reshape(2 * heads, features),
        dt_bias,
    )
    projected = jnp.einsum("td,dkf->ktf", whole, in_weight, preferred_element_type=F32)
    own, arrived = pl.pallas_call(
        functools.partial(mixer_kernel, outer, n),
        out_shape=(
            jax.ShapeDtypeStruct((length, columns), BF16),
            jax.ShapeDtypeStruct((n - 1, length, columns), BF16),
        ),
        in_specs=[anywhere, vmem, vmem, vmem, vmem, anywhere],
        out_specs=(vmem, vmem),
        scratch_shapes=[
            pltpu.VMEM((length, width), F32),
            pltpu.VMEM((length, width), F32),
            pltpu.VMEM(out_weight.shape, BF16),
            pltpu.VMEM((chunks, CHUNK, 2 * width), BF16),
            pltpu.VMEM((chunks, STATE, CHUNK), BF16),
            pltpu.VMEM((chunks, STATE, 2 * width), BF16),
            pltpu.VMEM((length, width), F32),
            pltpu.VMEM((GROUP, 2, STATE, quarter), BF16),
            pltpu.VMEM((GROUP, 2, 8, quarter), F32),
            pltpu.VMEM((GROUP, 2, STATE, quarter), BF16),
            pltpu.VMEM((GROUP, 2, 8, quarter), F32),
            pltpu.VMEM((GROUP, 2, STATE, quarter), F32),
            pltpu.VMEM((2, STATE, quarter), BF16),
            pltpu.VMEM((2, 8, quarter), F32),
            pltpu.VMEM((outer, STATE, quarter), BF16),
            pltpu.VMEM((outer, 8, quarter), F32),
            pltpu.VMEM((GROUP, 2, STATE, quarter), BF16),
            pltpu.VMEM((GROUP, 2, STATE, quarter), BF16),
            pltpu.VMEM((length, width), BF16),
            pltpu.VMEM((n - 1, length, columns), BF16),
        ]
        + [dma(((PARTS + 1) * (GROUP - 1),))] * 2
        + [dma(((PARTS + 1) * (outer - 1),))] * 2
        + [dma((PARTS * (GROUP - 1),))] * 2
        + [dma((chunks // 2 * (n - 1),))] * 2
        + [dma((3,))],
        compiler_params=pltpu.CompilerParams(
            vmem_limit_bytes=VMEM_LIMIT, collective_id=1, has_side_effects=True
        ),
        name="mixer",
    )(projected, both, raw, decay_rate[None], skip_gain[None], out_weight)
    total = own.astype(F32)
    for d in range(n - 1):
        total = total + arrived[d].astype(F32)
    return total.astype(BF16)


def solution(mesh):
    in_specs = (
        P("seq", "tp"),
        P(None, None, "tp"),
        P(None, "tp"),
        P(None, None, "tp"),
        P(None, "tp"),
        P("tp"),
        P("tp"),
        P("tp", None),
    )
    out_specs = P("seq", "tp")
    return jax.shard_map(shards, mesh=mesh, in_specs=in_specs, out_specs=out_specs, check_vma=False)
```

```python
import functools

import jax
import jax.numpy as jnp
from jax import lax
from jax.experimental import pallas as pl
from jax.experimental.pallas import tpu as pltpu
from jax.sharding import PartitionSpec as P

HEAD_DIM = 64
STATE = 128
CHUNK = 128
GROUP = 4
PARTS = 4
VMEM_LIMIT = 40 * 1024 * 1024
GATHER_LIMIT = 60 * 1024 * 1024
LOG2_E = 1.4426950408889634
F32 = jnp.float32
BF16 = jnp.bfloat16
HIGH = lax.Precision.HIGHEST


def dot(a, b, contract=((1,), (0,)), precision=None):
    return lax.dot_general(
        a, b, (contract, ((), ())), precision=precision, preferred_element_type=F32
    )


def split_wide(value):
    high = value.astype(BF16)
    return jnp.concatenate([high, (value - high.astype(F32)).astype(BF16)], axis=1)


def spread_matrix(count, dtype, copies=1):
    rows = lax.broadcasted_iota(jnp.int32, (copies * count, count * HEAD_DIM), 0)
    lanes = lax.broadcasted_iota(jnp.int32, (copies * count, count * HEAD_DIM), 1)
    return (lax.rem(rows, count) == lanes // HEAD_DIM).astype(dtype)


def gather_kernel(n, tokens_ref, bc_ref, dt_ref, bias_ref, whole_ref, both_ref, raw_ref, *scratch):
    columns, dt, send_bc, recv_bc, send_tok, recv_tok, here_sem = scratch
    me = lax.axis_index("tp")
    width = tokens_ref.shape[1]

    def features(owner):
        return pl.ds(pl.multiple_of(owner * width, width), width)

    own_bc = pltpu.make_async_copy(bc_ref, columns.at[me], here_sem.at[0])
    own_tokens = pltpu.make_async_copy(tokens_ref, whole_ref.at[:, features(me)], here_sem.at[1])
    own_dt = pltpu.make_async_copy(dt_ref, dt, here_sem.at[2])
    barrier = pltpu.get_barrier_semaphore()
    for d in range(1, n):
        pl.semaphore_signal(
            barrier, inc=1, device_id={"tp": (me + d) % n}, device_id_type=pl.DeviceIdType.MESH
        )
    own_bc.start()
    own_tokens.start()
    own_dt.start()
    pl.semaphore_wait(barrier, n - 1)
    weights, parts = [], []
    for d in range(1, n):
        to = {"tp": (me + d) % n}
        weights.append(
            pltpu.make_async_remote_copy(
                src_ref=bc_ref,
                dst_ref=columns.at[me],
                send_sem=send_bc.at[d - 1],
                recv_sem=recv_bc.at[d - 1],
                device_id=to,
                device_id_type=pl.DeviceIdType.MESH,
            )
        )
        parts.append(
            pltpu.make_async_remote_copy(
                src_ref=tokens_ref,
                dst_ref=whole_ref.at[:, features(me)],
                send_sem=send_tok.at[d - 1],
                recv_sem=recv_tok.at[d - 1],
                device_id=to,
                device_id_type=pl.DeviceIdType.MESH,
            )
        )
    for copy in weights + parts:
        copy.start()
    own_bc.wait()
    own_tokens.wait()
    own_dt.wait()
    for copy in weights:
        copy.wait()
    both = None
    raw = jnp.concatenate([bias_ref[:1, :], bias_ref[1:, :]], axis=1)
    for d in range(n):
        if d:
            parts[d - 1].wait()
        here = features((me + n - d) % n)
        part = whole_ref[:, here]
        new = jnp.concatenate([dot(part, columns[s, here, :]) for s in range(n)], axis=1)
        both = new if both is None else both + new
        raw = raw + dot(part, dt[:, here], ((1,), (1,)))
    both_ref[...] = both.astype(BF16)
    raw_ref[...] = raw


def mixer_kernel(
    outer,
    n,
    proj_ref,
    both_ref,
    raw_ref,
    rate_ref,
    gain_ref,
    weight_hbm,
    own,
    arrived,
    values_wide,
    gates,
    weight_ref,
    weighted,
    turned,
    local,
    mix,
    send_ref,
    total_ref,
    got,
    got_total,
    inner,
    group,
    group_total,
    far,
    far_total,
    back,
    landed,
    hidden,
    scales,
    leaving,
    send1,
    recv1,
    send2,
    recv2,
    send3,
    recv3,
    send4,
    recv4,
    here_sem,
):
    seq = lax.axis_index("seq")
    me = lax.axis_index("tp")
    z, g = seq // GROUP, seq % GROUP
    heads2 = raw_ref.shape[1]
    heads = heads2 // 2
    width = heads * HEAD_DIM
    chunks = raw_ref.shape[0] // CHUNK
    quarter = width // GROUP
    columns = own.shape[1]

    get_values = []
    for c in range(chunks):
        rows = pl.ds(c * CHUNK, CHUNK)
        source = proj_ref.at[0, rows, :]
        get_values.append(pltpu.make_async_copy(source, values_wide.at[rows, :], here_sem.at[c]))
        get_values[c].start()
    get_gates = pltpu.make_async_copy(proj_ref.at[1], gates, here_sem.at[chunks])
    get_weight = pltpu.make_async_copy(weight_hbm, weight_ref, here_sem.at[chunks + 1])
    get_gates.start()
    get_weight.start()

    def peer(zz, gg):
        return {"seq": zz * GROUP + gg}

    barrier = pltpu.get_barrier_semaphore()
    friends = [peer(z, (g + d) % GROUP) for d in range(1, GROUP)]
    friends += [peer((z + d) % outer, g) for d in range(1, outer)]
    friends += [{"tp": (me + d) % n} for d in range(1, n)]
    for friend in friends:
        pl.semaphore_signal(barrier, inc=1, device_id=friend, device_id_type=pl.DeviceIdType.MESH)

    def push(source, target, sends, recvs, slot, where):
        copy = pltpu.make_async_remote_copy(
            src_ref=source,
            dst_ref=target,
            send_sem=sends.at[slot],
            recv_sem=recvs.at[slot],
            device_id=where,
            device_id_type=pl.DeviceIdType.MESH,
        )
        copy.start()
        return copy

    every = chunks * heads2
    raw = jnp.concatenate(
        [raw_ref[c * CHUNK : (c + 1) * CHUNK, :] for c in range(chunks)], axis=1
    )
    rate = jnp.concatenate([rate_ref[...]] * (2 * chunks), axis=1)
    steps = jnp.maximum(raw, 0.0) + jnp.log1p(jnp.exp(-jnp.abs(raw)))
    logs = -rate * steps
    rows_of = lax.broadcasted_iota(jnp.int32, (CHUNK, CHUNK), 0)
    cols_of = lax.broadcasted_iota(jnp.int32, (CHUNK, CHUNK), 1)
    upto = dot((rows_of >= cols_of).astype(F32), logs, precision=HIGH)
    before = upto - logs
    last = upto[CHUNK - 1 : CHUNK, :]
    forward = lax.rem(lax.broadcasted_iota(jnp.int32, (CHUNK, every), 1), heads2) < heads
    weight = jnp.exp(jnp.where(forward, last - upto, before)) * steps
    column = LOG2_E * jnp.where(forward, before, -upto)
    row = (LOG2_E * (jnp.where(forward, -upto, before) + jnp.log(steps))).T
    scale = jnp.exp(jnp.where(forward, before, last - upto))
    lasts = [last[:, c * heads2 : (c + 1) * heads2] for c in range(chunks)]
    passed = []
    for c in range(chunks):
        gone = jnp.zeros((1, heads2), F32)
        for other in range(chunks):
            if other < c:
                gone = gone + jnp.where(forward[:1, :heads2], lasts[other], 0.0)
            if other > c:
                gone = gone + jnp.where(forward[:1, :heads2], 0.0, lasts[other])
        passed.append(gone)
    enter_scale = scale * jnp.exp(jnp.concatenate(passed, axis=1))
    spread = spread_matrix(heads2, BF16, 2)
    spread_one = spread_matrix(heads, BF16, 2)
    stack = lasts + [functools.reduce(jnp.add, lasts)]
    stack = stack + [jnp.zeros((1, heads2), F32)] * (8 - len(stack))
    totals = dot(jnp.concatenate(stack, axis=0), spread_matrix(heads2, F32), precision=HIGH)
    gain = jnp.broadcast_to(gain_ref[...], (8, heads))
    gain = dot(gain, spread_matrix(heads, F32), precision=HIGH)[:1]

    def spread_chunk(value, c):
        return dot(split_wide(value[:, c * heads2 : (c + 1) * heads2]), spread)

    for c in range(chunks):
        get_values[c].wait()
        rows = slice(c * CHUNK, (c + 1) * CHUNK)
        values = values_wide[rows, :].astype(BF16).astype(F32)
        wide = jnp.concatenate([values, values], axis=1) * spread_chunk(weight, c)
        weighted[c] = wide.astype(BF16)
        turned[c] = both_ref[rows, :STATE].T

    def block_state(rows):
        for way in range(2):
            side = slice(way * width, (way + 1) * width)
            carry = jnp.zeros((rows.stop - rows.start, width), F32)
            for c in range(chunks) if way == 0 else range(chunks - 1, -1, -1):
                local[c, rows, side] = carry.astype(BF16)
                new = dot(turned[c, rows, :], weighted[c, :, side])
                carry = jnp.exp(totals[c : c + 1, side]) * carry + new
            for q in range(GROUP):
                part = slice(q * quarter, (q + 1) * quarter)
                send_ref[q, way, rows, :] = carry[:, part].astype(BF16)

    for way in range(2):
        for q in range(GROUP):
            part = slice(way * width + q * quarter, way * width + (q + 1) * quarter)
            total_ref[q, way] = jnp.broadcast_to(totals[chunks : chunks + 1, part], (8, quarter))

    bands = [pl.ds(p * (STATE // PARTS), STATE // PARTS) for p in range(PARTS)]
    first = [[] for _ in bands]
    second = [[] for _ in bands]
    third = []
    before_state = [[None] * GROUP, [None] * GROUP]

    def share(p):
        for d in range(1, GROUP):
            to = (g + d) % GROUP
            if p == 0:
                total = total_ref.at[to]
                first[p].append(push(total, got_total.at[g], send1, recv1, d - 1, peer(z, to)))
            slot = (p + 1) * (GROUP - 1) + d - 1
            source = send_ref.at[to, :, bands[p], :]
            target = got.at[g, :, bands[p], :]
            first[p].append(push(source, target, send1, recv1, slot, peer(z, to)))

    def along(p):
        band = bands[p]
        for copy in first[p]:
            copy.wait()
        for way in range(2):
            carry = jnp.zeros((STATE // PARTS, quarter), F32)
            gone = jnp.zeros((8, quarter), F32)
            for s in range(GROUP) if way == 0 else range(GROUP - 1, -1, -1):
                inner[s, way, band, :] = carry
                before_state[way][s] = jnp.exp(gone[:1])
                carry = jnp.exp(got_total[s, way][:1]) * carry + got[s, way, band, :].astype(F32)
                gone = gone + got_total[s, way]
            group[way, band, :] = carry.astype(BF16)
            if p == 0:
                group_total[way] = gone
        for d in range(1, outer):
            way = (z + d) // outer
            to = peer((z + d) % outer, g)
            if p == 0:
                total = group_total.at[way]
                second[p].append(push(total, far_total.at[z], send2, recv2, d - 1, to))
            slot = (p + 1) * (outer - 1) + d - 1
            source = group.at[way, band, :]
            second[p].append(push(source, far.at[z, band, :], send2, recv2, slot, to))

    def hand_back(p):
        band = bands[p]
        for copy in second[p]:
            copy.wait()
        for way in range(2):
            carry = jnp.zeros((STATE // PARTS, quarter), F32)
            for s in range(outer) if way == 0 else range(outer - 1, -1, -1):
                longer = jnp.exp(far_total[s][:1]) * carry + far[s, band, :].astype(F32)
                carry = jnp.where(s < z if way == 0 else s > z, longer, carry)
            for s in range(GROUP):
                entering = inner[s, way, band, :] + before_state[way][s] * carry
                back[s, way, band, :] = entering.astype(BF16)
        for d in range(1, GROUP):
            to = (g + d) % GROUP
            slot = p * (GROUP - 1) + d - 1
            source = back.at[to, :, band, :]
            third.append(push(source, landed.at[g, :, band, :], send3, recv3, slot, peer(z, to)))

    half = STATE // 2
    block_state(slice(0, half))
    pl.semaphore_wait(barrier, GROUP - 1 + outer - 1 + n - 1)
    share(0)
    share(1)
    block_state(slice(half, STATE))
    share(2)
    share(3)
    got[g] = send_ref[g]
    got_total[g] = total_ref[g]
    far[z] = jnp.zeros(far.shape[1:], BF16)
    far_total[z] = jnp.zeros(far_total.shape[1:], F32)

    lower = rows_of > cols_of
    on_line = rows_of == cols_of
    first_half = lax.broadcasted_iota(jnp.int32, (CHUNK, 2 * HEAD_DIM), 1) < HEAD_DIM

    def inside(c):
        rows = slice(c * CHUNK, (c + 1) * CHUNK)
        scores = dot(both_ref[rows, STATE:], both_ref[rows, :STATE], ((1,), (1,)))
        for pair in range(heads // 2):
            weights = []
            for h in (2 * pair, 2 * pair + 1):
                f = c * heads2 + h
                b = f + heads
                power = jnp.where(
                    lower,
                    column[:, f : f + 1] + row[f : f + 1, :],
                    column[:, b : b + 1] + row[b : b + 1, :],
                )
                power = jnp.where(on_line, -jnp.inf, power)
                weights.append((scores * jnp.exp2(power)).astype(BF16))
            lanes = slice(pair * 2 * HEAD_DIM, (pair + 1) * 2 * HEAD_DIM)
            pair_values = values_wide[rows, lanes].astype(BF16)
            zero = jnp.zeros_like(pair_values)
            stacked = jnp.concatenate(
                [
                    jnp.where(first_half, pair_values, zero),
                    jnp.where(first_half, zero, pair_values),
                ],
                axis=0,
            )
            mix[rows, lanes] = dot(jnp.concatenate(weights, axis=1), stacked)

    def nearby(c):
        rows = slice(c * CHUNK, (c + 1) * CHUNK)
        reach = dot(both_ref[rows, STATE:], local[c]) * spread_chunk(scale, c)
        values = values_wide[rows, :].astype(BF16).astype(F32)
        mix[rows, :] = mix[rows, :] + reach[:, :width] + reach[:, width:] + gain * values

    def activate(c):
        rows = slice(c * CHUNK, (c + 1) * CHUNK)
        gates[rows, :] = gates[rows, :] / (1.0 + jnp.exp(-gates[rows, :]))

    def spread_scale(c):
        scales[c] = spread_chunk(enter_scale, c)

    inside(0)
    along(0)
    along(1)
    inside(1)
    along(2)
    along(3)
    hand_back(0)
    inside(2)
    hand_back(1)
    hand_back(2)
    inside(3)
    hand_back(3)
    landed[g] = back[g]
    get_gates.wait()
    for c in range(chunks):
        nearby(c)
        activate(c)
        spread_scale(c)
    get_weight.wait()
    for copy in third:
        copy.wait()

    copies = []
    for c in range(chunks):
        rows = slice(c * CHUNK, (c + 1) * CHUNK)
        queries = both_ref[rows, STATE:]
        reach = [dot(queries, landed[q, way]) for way in range(2) for q in range(GROUP)]
        reach = jnp.concatenate(reach, axis=1) * scales[c]
        gated = (mix[rows, :] + reach[:, :width] + reach[:, width:]) * gates[rows, :]
        square = gated * gated
        high = square.astype(BF16)
        low = (square - high.astype(F32)).astype(BF16)
        unit = spread_one[:heads]
        power = dot(high, unit, ((1,), (1,))) + dot(low, unit, ((1,), (1,)))
        norm = lax.rsqrt(power * (1.0 / HEAD_DIM) + 1e-05)
        hidden[rows, :] = (gated * dot(split_wide(norm), spread_one)).astype(BF16)
        if c % 2 == 0:
            continue
        rows = slice((c - 1) * CHUNK, (c + 1) * CHUNK)
        for d in range(1, n):
            to = (me + d) % n
            theirs = pl.ds(pl.multiple_of(to * columns, columns), columns)
            leaving[d - 1, rows, :] = dot(hidden[rows, :], weight_ref[:, theirs]).astype(BF16)
            slot = c // 2 * (n - 1) + d - 1
            source = leaving.at[d - 1, rows, :]
            copies.append(
                push(source, arrived.at[d - 1, rows, :], send4, recv4, slot, {"tp": to})
            )
    mine = pl.ds(pl.multiple_of(me * columns, columns), columns)
    own[...] = dot(hidden[...], weight_ref[:, mine]).astype(BF16)
    for copy in copies:
        copy.wait()


def shards(tokens, in_weight, bc_weight, dt_weight, dt_bias, decay_rate, skip_gain, out_weight):
    heads = decay_rate.shape[0]
    width = heads * HEAD_DIM
    quarter = width // GROUP
    outer = lax.axis_size("seq") // GROUP
    n = lax.axis_size("tp")
    length = tokens.shape[0]
    features = dt_weight.shape[1]
    chunks = length // CHUNK
    columns = out_weight.shape[1] // n
    vmem = pl.BlockSpec(memory_space=pltpu.VMEM)
    anywhere = pl.BlockSpec(memory_space=pl.ANY)
    dma = pltpu.SemaphoreType.DMA
    whole, both, raw = pl.pallas_call(
        functools.partial(gather_kernel, n),
        out_shape=(
            jax.ShapeDtypeStruct((length, features), BF16),
            jax.ShapeDtypeStruct((length, 2 * STATE), BF16),
            jax.ShapeDtypeStruct((length, 2 * heads), F32),
        ),
        in_specs=[pl.BlockSpec(memory_space=pltpu.HBM)] * 3 + [vmem],
        out_specs=(vmem, vmem, vmem),
        scratch_shapes=[
            pltpu.VMEM((n,) + bc_weight.shape, BF16),
            pltpu.VMEM((2 * heads, features), BF16),
        ]
        + [dma((n - 1,))] * 4
        + [dma((3,))],
        compiler_params=pltpu.CompilerParams(
            vmem_limit_bytes=GATHER_LIMIT, collective_id=0, has_side_effects=True
        ),
        name="gather_features",
    )(
        tokens,
        bc_weight,
        dt_weight.transpose(0, 2, 1).reshape(2 * heads, features),
        dt_bias,
    )
    projected = jnp.einsum("td,dkf->ktf", whole, in_weight, preferred_element_type=F32)
    own, arrived = pl.pallas_call(
        functools.partial(mixer_kernel, outer, n),
        out_shape=(
            jax.ShapeDtypeStruct((length, columns), BF16),
            jax.ShapeDtypeStruct((n - 1, length, columns), BF16),
        ),
        in_specs=[anywhere, vmem, vmem, vmem, vmem, anywhere],
        out_specs=(vmem, vmem),
        scratch_shapes=[
            pltpu.VMEM((length, width), F32),
            pltpu.VMEM((length, width), F32),
            pltpu.VMEM(out_weight.shape, BF16),
            pltpu.VMEM((chunks, CHUNK, 2 * width), BF16),
            pltpu.VMEM((chunks, STATE, CHUNK), BF16),
            pltpu.VMEM((chunks, STATE, 2 * width), BF16),
            pltpu.VMEM((length, width), F32),
            pltpu.VMEM((GROUP, 2, STATE, quarter), BF16),
            pltpu.VMEM((GROUP, 2, 8, quarter), F32),
            pltpu.VMEM((GROUP, 2, STATE, quarter), BF16),
            pltpu.VMEM((GROUP, 2, 8, quarter), F32),
            pltpu.VMEM((GROUP, 2, STATE, quarter), F32),
            pltpu.VMEM((2, STATE, quarter), BF16),
            pltpu.VMEM((2, 8, quarter), F32),
            pltpu.VMEM((outer, STATE, quarter), BF16),
            pltpu.VMEM((outer, 8, quarter), F32),
            pltpu.VMEM((GROUP, 2, STATE, quarter), BF16),
            pltpu.VMEM((GROUP, 2, STATE, quarter), BF16),
            pltpu.VMEM((length, width), BF16),
            pltpu.VMEM((chunks, CHUNK, 2 * width), F32),
            pltpu.VMEM((n - 1, length, columns), BF16),
        ]
        + [dma(((PARTS + 1) * (GROUP - 1),))] * 2
        + [dma(((PARTS + 1) * (outer - 1),))] * 2
        + [dma((PARTS * (GROUP - 1),))] * 2
        + [dma((chunks // 2 * (n - 1),))] * 2
        + [dma((chunks + 2,))],
        compiler_params=pltpu.CompilerParams(
            vmem_limit_bytes=VMEM_LIMIT, collective_id=1, has_side_effects=True
        ),
        name="mixer",
    )(projected, both, raw, decay_rate[None], skip_gain[None], out_weight)
    total = own.astype(F32)
    for d in range(n - 1):
        total = total + arrived[d].astype(F32)
    return total.astype(BF16)


def solution(mesh):
    in_specs = (
        P("seq", "tp"),
        P(None, None, "tp"),
        P(None, "tp"),
        P(None, None, "tp"),
        P(None, "tp"),
        P("tp"),
        P("tp"),
        P("tp", None),
    )
    out_specs = P("seq", "tp")
    return jax.shard_map(shards, mesh=mesh, in_specs=in_specs, out_specs=out_specs, check_vma=False)
```

```python
import functools

import jax
import jax.numpy as jnp
from jax import lax
from jax.experimental import pallas as pl
from jax.experimental.pallas import tpu as pltpu
from jax.sharding import PartitionSpec as P

HEAD_DIM = 64
STATE = 128
CHUNK = 128
GROUP = 4
PARTS = 4
VMEM_LIMIT = 40 * 1024 * 1024
GATHER_LIMIT = 60 * 1024 * 1024
LOG2_E = 1.4426950408889634
F32 = jnp.float32
BF16 = jnp.bfloat16
HIGH = lax.Precision.HIGHEST


def dot(a, b, contract=((1,), (0,)), precision=None):
    return lax.dot_general(
        a, b, (contract, ((), ())), precision=precision, preferred_element_type=F32
    )


def split_wide(value):
    high = value.astype(BF16)
    return jnp.concatenate([high, (value - high.astype(F32)).astype(BF16)], axis=1)


def spread_matrix(count, dtype, copies=1):
    rows = lax.broadcasted_iota(jnp.int32, (copies * count, count * HEAD_DIM), 0)
    lanes = lax.broadcasted_iota(jnp.int32, (copies * count, count * HEAD_DIM), 1)
    return (lax.rem(rows, count) == lanes // HEAD_DIM).astype(dtype)


def gather_kernel(n, tokens_ref, bc_ref, dt_ref, bias_ref, whole_ref, both_ref, raw_ref, *scratch):
    columns, dt, mine, came, send_bc, recv_bc, send_tok, recv_tok, here_sem, back_sem = scratch
    me = lax.axis_index("tp")
    length, width = tokens_ref.shape
    bands = [pl.ds(r * (length // 2), length // 2) for r in range(2)]

    def features(owner):
        return pl.ds(pl.multiple_of(owner * width, width), width)

    own_bc = pltpu.make_async_copy(bc_ref, columns.at[me], here_sem.at[0])
    own_tokens = pltpu.make_async_copy(tokens_ref, mine, here_sem.at[1])
    own_part = pltpu.make_async_copy(tokens_ref, whole_ref.at[:, features(me)], here_sem.at[3])
    own_dt = pltpu.make_async_copy(dt_ref, dt, here_sem.at[2])
    barrier = pltpu.get_barrier_semaphore()
    for d in range(1, n):
        pl.semaphore_signal(
            barrier, inc=1, device_id={"tp": (me + d) % n}, device_id_type=pl.DeviceIdType.MESH
        )
    own_bc.start()
    own_tokens.start()
    own_dt.start()
    pl.semaphore_wait(barrier, n - 1)
    weights, parts = [], []
    for d in range(1, n):
        to = {"tp": (me + d) % n}
        weights.append(
            pltpu.make_async_remote_copy(
                src_ref=bc_ref,
                dst_ref=columns.at[me],
                send_sem=send_bc.at[d - 1],
                recv_sem=recv_bc.at[d - 1],
                device_id=to,
                device_id_type=pl.DeviceIdType.MESH,
            )
        )
        for r, band in enumerate(bands):
            parts.append(
                pltpu.make_async_remote_copy(
                    src_ref=tokens_ref.at[band, :],
                    dst_ref=came.at[d - 1, band, :],
                    send_sem=send_tok.at[2 * d - 2 + r],
                    recv_sem=recv_tok.at[2 * d - 2 + r],
                    device_id=to,
                    device_id_type=pl.DeviceIdType.MESH,
                )
            )
    for copy in weights + parts:
        copy.start()
    own_part.start()
    own_bc.wait()
    own_tokens.wait()
    own_dt.wait()
    for copy in weights:
        copy.wait()

    def products(part, owner):
        here = features(owner)
        new = jnp.concatenate([dot(part, columns[s, here, :]) for s in range(n)], axis=1)
        return new, dot(part, dt[:, here], ((1,), (1,)))

    own_both, own_raw = products(mine[...], me)
    bias = jnp.concatenate([bias_ref[:1, :], bias_ref[1:, :]], axis=1)
    backs = [own_part]
    for r, band in enumerate(bands):
        both = own_both[r * (length // 2) : (r + 1) * (length // 2), :]
        raw = own_raw[r * (length // 2) : (r + 1) * (length // 2), :] + bias
        for d in range(1, n):
            owner = (me + n - d) % n
            slot = 2 * d - 2 + r
            parts[slot].wait()
            source = came.at[d - 1, band, :]
            target = whole_ref.at[band, features(owner)]
            backs.append(pltpu.make_async_copy(source, target, back_sem.at[slot]))
            backs[-1].start()
            new_both, new_raw = products(came[d - 1, band, :], owner)
            both = both + new_both
            raw = raw + new_raw
        both_ref[band, :] = both.astype(BF16)
        raw_ref[band, :] = raw
    for copy in backs:
        copy.wait()


def mixer_kernel(
    outer,
    n,
    proj_ref,
    both_ref,
    raw_ref,
    rate_ref,
    gain_ref,
    weight_hbm,
    own,
    arrived,
    values_wide,
    gates,
    weight_ref,
    weighted,
    turned,
    local,
    mix,
    send_ref,
    total_ref,
    got,
    got_total,
    inner,
    group,
    group_total,
    far,
    far_total,
    back,
    landed,
    hidden,
    scales,
    leaving,
    send1,
    recv1,
    send2,
    recv2,
    send3,
    recv3,
    send4,
    recv4,
    here_sem,
):
    seq = lax.axis_index("seq")
    me = lax.axis_index("tp")
    z, g = seq // GROUP, seq % GROUP
    heads2 = raw_ref.shape[1]
    heads = heads2 // 2
    width = heads * HEAD_DIM
    chunks = raw_ref.shape[0] // CHUNK
    quarter = width // GROUP
    columns = own.shape[1]

    get_values = []
    for c in range(chunks):
        rows = pl.ds(c * CHUNK, CHUNK)
        source = proj_ref.at[0, rows, :]
        get_values.append(pltpu.make_async_copy(source, values_wide.at[rows, :], here_sem.at[c]))
        get_values[c].start()
    get_gates = pltpu.make_async_copy(proj_ref.at[1], gates, here_sem.at[chunks])
    get_weight = pltpu.make_async_copy(weight_hbm, weight_ref, here_sem.at[chunks + 1])
    get_gates.start()
    get_weight.start()

    def peer(zz, gg):
        return {"seq": zz * GROUP + gg}

    barrier = pltpu.get_barrier_semaphore()
    friends = [peer(z, (g + d) % GROUP) for d in range(1, GROUP)]
    friends += [peer((z + d) % outer, g) for d in range(1, outer)]
    friends += [{"tp": (me + d) % n} for d in range(1, n)]
    for friend in friends:
        pl.semaphore_signal(barrier, inc=1, device_id=friend, device_id_type=pl.DeviceIdType.MESH)

    def push(source, target, sends, recvs, slot, where):
        copy = pltpu.make_async_remote_copy(
            src_ref=source,
            dst_ref=target,
            send_sem=sends.at[slot],
            recv_sem=recvs.at[slot],
            device_id=where,
            device_id_type=pl.DeviceIdType.MESH,
        )
        copy.start()
        return copy

    every = chunks * heads2
    raw = jnp.concatenate(
        [raw_ref[c * CHUNK : (c + 1) * CHUNK, :] for c in range(chunks)], axis=1
    )
    rate = jnp.concatenate([rate_ref[...]] * (2 * chunks), axis=1)
    steps = jnp.maximum(raw, 0.0) + jnp.log1p(jnp.exp(-jnp.abs(raw)))
    logs = -rate * steps
    rows_of = lax.broadcasted_iota(jnp.int32, (CHUNK, CHUNK), 0)
    cols_of = lax.broadcasted_iota(jnp.int32, (CHUNK, CHUNK), 1)
    upto = dot((rows_of >= cols_of).astype(F32), logs, precision=HIGH)
    before = upto - logs
    last = upto[CHUNK - 1 : CHUNK, :]
    forward = lax.rem(lax.broadcasted_iota(jnp.int32, (CHUNK, every), 1), heads2) < heads
    weight = jnp.exp(jnp.where(forward, last - upto, before)) * steps
    column = LOG2_E * jnp.where(forward, before, -upto)
    row = (LOG2_E * (jnp.where(forward, -upto, before) + jnp.log(steps))).T
    scale = jnp.exp(jnp.where(forward, before, last - upto))
    lasts = [last[:, c * heads2 : (c + 1) * heads2] for c in range(chunks)]
    passed = []
    for c in range(chunks):
        gone = jnp.zeros((1, heads2), F32)
        for other in range(chunks):
            if other < c:
                gone = gone + jnp.where(forward[:1, :heads2], lasts[other], 0.0)
            if other > c:
                gone = gone + jnp.where(forward[:1, :heads2], 0.0, lasts[other])
        passed.append(gone)
    enter_scale = scale * jnp.exp(jnp.concatenate(passed, axis=1))
    spread = spread_matrix(heads2, BF16, 2)
    spread_one = spread_matrix(heads, BF16, 2)
    stack = lasts + [functools.reduce(jnp.add, lasts)]
    stack = stack + [jnp.zeros((1, heads2), F32)] * (8 - len(stack))
    totals = dot(jnp.concatenate(stack, axis=0), spread_matrix(heads2, F32), precision=HIGH)
    gain = jnp.broadcast_to(gain_ref[...], (8, heads))
    gain = dot(gain, spread_matrix(heads, F32), precision=HIGH)[:1]

    def spread_chunk(value, c):
        return dot(split_wide(value[:, c * heads2 : (c + 1) * heads2]), spread)

    for c in range(chunks):
        get_values[c].wait()
        rows = slice(c * CHUNK, (c + 1) * CHUNK)
        values = values_wide[rows, :].astype(BF16).astype(F32)
        wide = jnp.concatenate([values, values], axis=1) * spread_chunk(weight, c)
        weighted[c] = wide.astype(BF16)
        turned[c] = both_ref[rows, :STATE].T

    def block_state(rows):
        for way in range(2):
            side = slice(way * width, (way + 1) * width)
            carry = jnp.zeros((rows.stop - rows.start, width), F32)
            for c in range(chunks) if way == 0 else range(chunks - 1, -1, -1):
                local[c, rows, side] = carry.astype(BF16)
                new = dot(turned[c, rows, :], weighted[c, :, side])
                carry = jnp.exp(totals[c : c + 1, side]) * carry + new
            for q in range(GROUP):
                part = slice(q * quarter, (q + 1) * quarter)
                send_ref[q, way, rows, :] = carry[:, part].astype(BF16)

    for way in range(2):
        for q in range(GROUP):
            part = slice(way * width + q * quarter, way * width + (q + 1) * quarter)
            total_ref[q, way] = jnp.broadcast_to(totals[chunks : chunks + 1, part], (8, quarter))

    bands = [pl.ds(p * (STATE // PARTS), STATE // PARTS) for p in range(PARTS)]
    first = [[] for _ in bands]
    second = [[] for _ in bands]
    third = []
    before_state = [[None] * GROUP, [None] * GROUP]

    def share(p):
        for d in range(1, GROUP):
            to = (g + d) % GROUP
            if p == 0:
                total = total_ref.at[to]
                first[p].append(push(total, got_total.at[g], send1, recv1, d - 1, peer(z, to)))
            slot = (p + 1) * (GROUP - 1) + d - 1
            source = send_ref.at[to, :, bands[p], :]
            target = got.at[g, :, bands[p], :]
            first[p].append(push(source, target, send1, recv1, slot, peer(z, to)))

    def along(p):
        band = bands[p]
        for copy in first[p]:
            copy.wait()
        for way in range(2):
            carry = jnp.zeros((STATE // PARTS, quarter), F32)
            gone = jnp.zeros((8, quarter), F32)
            for s in range(GROUP) if way == 0 else range(GROUP - 1, -1, -1):
                inner[s, way, band, :] = carry
                before_state[way][s] = jnp.exp(gone[:1])
                carry = jnp.exp(got_total[s, way][:1]) * carry + got[s, way, band, :].astype(F32)
                gone = gone + got_total[s, way]
            group[way, band, :] = carry.astype(BF16)
            if p == 0:
                group_total[way] = gone
        for d in range(1, outer):
            way = (z + d) // outer
            to = peer((z + d) % outer, g)
            if p == 0:
                total = group_total.at[way]
                second[p].append(push(total, far_total.at[z], send2, recv2, d - 1, to))
            slot = (p + 1) * (outer - 1) + d - 1
            source = group.at[way, band, :]
            second[p].append(push(source, far.at[z, band, :], send2, recv2, slot, to))

    def hand_back(p):
        band = bands[p]
        for copy in second[p]:
            copy.wait()
        for way in range(2):
            carry = jnp.zeros((STATE // PARTS, quarter), F32)
            for s in range(outer) if way == 0 else range(outer - 1, -1, -1):
                longer = jnp.exp(far_total[s][:1]) * carry + far[s, band, :].astype(F32)
                carry = jnp.where(s < z if way == 0 else s > z, longer, carry)
            for s in range(GROUP):
                entering = inner[s, way, band, :] + before_state[way][s] * carry
                back[s, way, band, :] = entering.astype(BF16)
        for d in range(1, GROUP):
            to = (g + d) % GROUP
            slot = p * (GROUP - 1) + d - 1
            source = back.at[to, :, band, :]
            third.append(push(source, landed.at[g, :, band, :], send3, recv3, slot, peer(z, to)))

    half = STATE // 2
    block_state(slice(0, half))
    pl.semaphore_wait(barrier, GROUP - 1 + outer - 1 + n - 1)
    share(0)
    share(1)
    block_state(slice(half, STATE))
    share(2)
    share(3)
    got[g] = send_ref[g]
    got_total[g] = total_ref[g]
    far[z] = jnp.zeros(far.shape[1:], BF16)
    far_total[z] = jnp.zeros(far_total.shape[1:], F32)

    lower = rows_of > cols_of
    on_line = rows_of == cols_of
    first_half = lax.broadcasted_iota(jnp.int32, (CHUNK, 2 * HEAD_DIM), 1) < HEAD_DIM

    def inside(c):
        rows = slice(c * CHUNK, (c + 1) * CHUNK)
        scores = dot(both_ref[rows, STATE:], both_ref[rows, :STATE], ((1,), (1,)))
        for pair in range(heads // 2):
            weights = []
            for h in (2 * pair, 2 * pair + 1):
                f = c * heads2 + h
                b = f + heads
                power = jnp.where(
                    lower,
                    column[:, f : f + 1] + row[f : f + 1, :],
                    column[:, b : b + 1] + row[b : b + 1, :],
                )
                power = jnp.where(on_line, -jnp.inf, power)
                weights.append((scores * jnp.exp2(power)).astype(BF16))
            lanes = slice(pair * 2 * HEAD_DIM, (pair + 1) * 2 * HEAD_DIM)
            pair_values = values_wide[rows, lanes].astype(BF16)
            zero = jnp.zeros_like(pair_values)
            stacked = jnp.concatenate(
                [
                    jnp.where(first_half, pair_values, zero),
                    jnp.where(first_half, zero, pair_values),
                ],
                axis=0,
            )
            mix[rows, lanes] = dot(jnp.concatenate(weights, axis=1), stacked)

    def nearby(c):
        rows = slice(c * CHUNK, (c + 1) * CHUNK)
        reach = dot(both_ref[rows, STATE:], local[c]) * spread_chunk(scale, c)
        values = values_wide[rows, :].astype(BF16).astype(F32)
        mix[rows, :] = mix[rows, :] + reach[:, :width] + reach[:, width:] + gain * values

    def activate(c):
        rows = slice(c * CHUNK, (c + 1) * CHUNK)
        gates[rows, :] = gates[rows, :] / (1.0 + jnp.exp(-gates[rows, :]))

    def spread_scale(c):
        scales[c] = spread_chunk(enter_scale, c)

    inside(0)
    along(0)
    along(1)
    inside(1)
    along(2)
    along(3)
    hand_back(0)
    inside(2)
    hand_back(1)
    hand_back(2)
    inside(3)
    hand_back(3)
    landed[g] = back[g]
    get_gates.wait()
    for c in range(chunks):
        nearby(c)
        activate(c)
        spread_scale(c)
    get_weight.wait()
    for copy in third:
        copy.wait()

    copies = []
    for c in range(chunks):
        rows = slice(c * CHUNK, (c + 1) * CHUNK)
        queries = both_ref[rows, STATE:]
        reach = [dot(queries, landed[q, way]) for way in range(2) for q in range(GROUP)]
        reach = jnp.concatenate(reach, axis=1) * scales[c]
        gated = (mix[rows, :] + reach[:, :width] + reach[:, width:]) * gates[rows, :]
        square = gated * gated
        high = square.astype(BF16)
        low = (square - high.astype(F32)).astype(BF16)
        unit = spread_one[:heads]
        power = dot(high, unit, ((1,), (1,))) + dot(low, unit, ((1,), (1,)))
        norm = lax.rsqrt(power * (1.0 / HEAD_DIM) + 1e-05)
        hidden[rows, :] = (gated * dot(split_wide(norm), spread_one)).astype(BF16)
        if c % 2 == 0:
            continue
        rows = slice((c - 1) * CHUNK, (c + 1) * CHUNK)
        for d in range(1, n):
            to = (me + d) % n
            theirs = pl.ds(pl.multiple_of(to * columns, columns), columns)
            leaving[d - 1, rows, :] = dot(hidden[rows, :], weight_ref[:, theirs]).astype(BF16)
            slot = c // 2 * (n - 1) + d - 1
            source = leaving.at[d - 1, rows, :]
            copies.append(
                push(source, arrived.at[d - 1, rows, :], send4, recv4, slot, {"tp": to})
            )
    mine = pl.ds(pl.multiple_of(me * columns, columns), columns)
    own[...] = dot(hidden[...], weight_ref[:, mine]).astype(BF16)
    for copy in copies:
        copy.wait()


def shards(tokens, in_weight, bc_weight, dt_weight, dt_bias, decay_rate, skip_gain, out_weight):
    heads = decay_rate.shape[0]
    width = heads * HEAD_DIM
    quarter = width // GROUP
    outer = lax.axis_size("seq") // GROUP
    n = lax.axis_size("tp")
    length = tokens.shape[0]
    features = dt_weight.shape[1]
    chunks = length // CHUNK
    columns = out_weight.shape[1] // n
    vmem = pl.BlockSpec(memory_space=pltpu.VMEM)
    anywhere = pl.BlockSpec(memory_space=pl.ANY)
    dma = pltpu.SemaphoreType.DMA
    whole, both, raw = pl.pallas_call(
        functools.partial(gather_kernel, n),
        out_shape=(
            jax.ShapeDtypeStruct((length, features), BF16),
            jax.ShapeDtypeStruct((length, 2 * STATE), BF16),
            jax.ShapeDtypeStruct((length, 2 * heads), F32),
        ),
        in_specs=[pl.BlockSpec(memory_space=pltpu.HBM)] * 3 + [vmem],
        out_specs=(anywhere, vmem, vmem),
        scratch_shapes=[
            pltpu.VMEM((n,) + bc_weight.shape, BF16),
            pltpu.VMEM((2 * heads, features), BF16),
            pltpu.VMEM(tokens.shape, BF16),
            pltpu.VMEM((n - 1,) + tokens.shape, BF16),
        ]
        + [dma((n - 1,))] * 2
        + [dma((2 * (n - 1),))] * 2
        + [dma((4,)), dma((2 * (n - 1),))],
        compiler_params=pltpu.CompilerParams(
            vmem_limit_bytes=GATHER_LIMIT, collective_id=0, has_side_effects=True
        ),
        name="gather_features",
    )(
        tokens,
        bc_weight,
        dt_weight.transpose(0, 2, 1).reshape(2 * heads, features),
        dt_bias,
    )
    projected = jnp.einsum("td,dkf->ktf", whole, in_weight, preferred_element_type=F32)
    own, arrived = pl.pallas_call(
        functools.partial(mixer_kernel, outer, n),
        out_shape=(
            jax.ShapeDtypeStruct((length, columns), BF16),
            jax.ShapeDtypeStruct((n - 1, length, columns), BF16),
        ),
        in_specs=[anywhere, vmem, vmem, vmem, vmem, anywhere],
        out_specs=(vmem, vmem),
        scratch_shapes=[
            pltpu.VMEM((length, width), F32),
            pltpu.VMEM((length, width), F32),
            pltpu.VMEM(out_weight.shape, BF16),
            pltpu.VMEM((chunks, CHUNK, 2 * width), BF16),
            pltpu.VMEM((chunks, STATE, CHUNK), BF16),
            pltpu.VMEM((chunks, STATE, 2 * width), BF16),
            pltpu.VMEM((length, width), F32),
            pltpu.VMEM((GROUP, 2, STATE, quarter), BF16),
            pltpu.VMEM((GROUP, 2, 8, quarter), F32),
            pltpu.VMEM((GROUP, 2, STATE, quarter), BF16),
            pltpu.VMEM((GROUP, 2, 8, quarter), F32),
            pltpu.VMEM((GROUP, 2, STATE, quarter), F32),
            pltpu.VMEM((2, STATE, quarter), BF16),
            pltpu.VMEM((2, 8, quarter), F32),
            pltpu.VMEM((outer, STATE, quarter), BF16),
            pltpu.VMEM((outer, 8, quarter), F32),
            pltpu.VMEM((GROUP, 2, STATE, quarter), BF16),
            pltpu.VMEM((GROUP, 2, STATE, quarter), BF16),
            pltpu.VMEM((length, width), BF16),
            pltpu.VMEM((chunks, CHUNK, 2 * width), F32),
            pltpu.VMEM((n - 1, length, columns), BF16),
        ]
        + [dma(((PARTS + 1) * (GROUP - 1),))] * 2
        + [dma(((PARTS + 1) * (outer - 1),))] * 2
        + [dma((PARTS * (GROUP - 1),))] * 2
        + [dma((chunks // 2 * (n - 1),))] * 2
        + [dma((chunks + 2,))],
        compiler_params=pltpu.CompilerParams(
            vmem_limit_bytes=VMEM_LIMIT, collective_id=1, has_side_effects=True
        ),
        name="mixer",
    )(projected, both, raw, decay_rate[None], skip_gain[None], out_weight)
    total = own.astype(F32)
    for d in range(n - 1):
        total = total + arrived[d].astype(F32)
    return total.astype(BF16)


def solution(mesh):
    in_specs = (
        P("seq", "tp"),
        P(None, None, "tp"),
        P(None, "tp"),
        P(None, None, "tp"),
        P(None, "tp"),
        P("tp"),
        P("tp"),
        P("tp", None),
    )
    out_specs = P("seq", "tp")
    return jax.shard_map(shards, mesh=mesh, in_specs=in_specs, out_specs=out_specs, check_vma=False)
```

```python
import functools

import jax
import jax.numpy as jnp
from jax import lax
from jax.experimental import pallas as pl
from jax.experimental.pallas import tpu as pltpu
from jax.sharding import PartitionSpec as P

HEAD_DIM = 64
STATE = 128
CHUNK = 128
GROUP = 4
PARTS = 4
VMEM_LIMIT = 40 * 1024 * 1024
GATHER_LIMIT = 60 * 1024 * 1024
LOG2_E = 1.4426950408889634
F32 = jnp.float32
BF16 = jnp.bfloat16
HIGH = lax.Precision.HIGHEST


def dot(a, b, contract=((1,), (0,)), precision=None):
    return lax.dot_general(
        a, b, (contract, ((), ())), precision=precision, preferred_element_type=F32
    )


def split_wide(value):
    high = value.astype(BF16)
    return jnp.concatenate([high, (value - high.astype(F32)).astype(BF16)], axis=1)


def spread_matrix(count, dtype, copies=1):
    rows = lax.broadcasted_iota(jnp.int32, (copies * count, count * HEAD_DIM), 0)
    lanes = lax.broadcasted_iota(jnp.int32, (copies * count, count * HEAD_DIM), 1)
    return (lax.rem(rows, count) == lanes // HEAD_DIM).astype(dtype)


def gather_kernel(n, tokens_ref, bc_ref, dt_ref, bias_ref, whole_ref, both_ref, raw_ref, *scratch):
    columns, dt, mine, came, send_bc, recv_bc, send_tok, recv_tok, here_sem, back_sem = scratch
    me = lax.axis_index("tp")
    length, width = tokens_ref.shape
    bands = [pl.ds(r * (length // 2), length // 2) for r in range(2)]

    def features(owner):
        return pl.ds(pl.multiple_of(owner * width, width), width)

    own_bc = pltpu.make_async_copy(bc_ref, columns.at[me], here_sem.at[0])
    own_tokens = pltpu.make_async_copy(tokens_ref, mine, here_sem.at[1])
    own_part = pltpu.make_async_copy(mine, whole_ref.at[:, features(me)], here_sem.at[3])
    own_dt = pltpu.make_async_copy(dt_ref, dt, here_sem.at[2])
    barrier = pltpu.get_barrier_semaphore()
    for d in range(1, n):
        pl.semaphore_signal(
            barrier, inc=1, device_id={"tp": (me + d) % n}, device_id_type=pl.DeviceIdType.MESH
        )
    own_bc.start()
    own_tokens.start()
    own_dt.start()
    pl.semaphore_wait(barrier, n - 1)
    weights, parts = [], []
    for d in range(1, n):
        to = {"tp": (me + d) % n}
        weights.append(
            pltpu.make_async_remote_copy(
                src_ref=bc_ref,
                dst_ref=columns.at[me],
                send_sem=send_bc.at[d - 1],
                recv_sem=recv_bc.at[d - 1],
                device_id=to,
                device_id_type=pl.DeviceIdType.MESH,
            )
        )
        for r, band in enumerate(bands):
            parts.append(
                pltpu.make_async_remote_copy(
                    src_ref=tokens_ref.at[band, :],
                    dst_ref=came.at[d - 1, band, :],
                    send_sem=send_tok.at[2 * d - 2 + r],
                    recv_sem=recv_tok.at[2 * d - 2 + r],
                    device_id=to,
                    device_id_type=pl.DeviceIdType.MESH,
                )
            )
    for copy in weights + parts:
        copy.start()
    own_tokens.wait()
    own_part.start()
    own_bc.wait()
    own_dt.wait()
    for copy in weights:
        copy.wait()

    def products(part, owner):
        here = features(owner)
        new = jnp.concatenate([dot(part, columns[s, here, :]) for s in range(n)], axis=1)
        return new, dot(part, dt[:, here], ((1,), (1,)))

    own_both, own_raw = products(mine[...], me)
    bias = jnp.concatenate([bias_ref[:1, :], bias_ref[1:, :]], axis=1)
    backs = [own_part]
    for r, band in enumerate(bands):
        both = own_both[r * (length // 2) : (r + 1) * (length // 2), :]
        raw = own_raw[r * (length // 2) : (r + 1) * (length // 2), :] + bias
        for d in range(1, n):
            owner = (me + n - d) % n
            slot = 2 * d - 2 + r
            parts[slot].wait()
            source = came.at[d - 1, band, :]
            target = whole_ref.at[band, features(owner)]
            backs.append(pltpu.make_async_copy(source, target, back_sem.at[slot]))
            backs[-1].start()
            new_both, new_raw = products(came[d - 1, band, :], owner)
            both = both + new_both
            raw = raw + new_raw
        both_ref[band, :] = both.astype(BF16)
        raw_ref[band, :] = raw
    for copy in backs:
        copy.wait()


def mixer_kernel(
    outer,
    n,
    proj_ref,
    both_ref,
    raw_ref,
    rate_ref,
    gain_ref,
    weight_hbm,
    own,
    arrived,
    values_wide,
    gates,
    weight_ref,
    weighted,
    turned,
    local,
    mix,
    send_ref,
    total_ref,
    got,
    got_total,
    inner,
    group,
    group_total,
    far,
    far_total,
    back,
    landed,
    hidden,
    scales,
    leaving,
    send1,
    recv1,
    send2,
    recv2,
    send3,
    recv3,
    send4,
    recv4,
    here_sem,
):
    seq = lax.axis_index("seq")
    me = lax.axis_index("tp")
    z, g = seq // GROUP, seq % GROUP
    heads2 = raw_ref.shape[1]
    heads = heads2 // 2
    width = heads * HEAD_DIM
    chunks = raw_ref.shape[0] // CHUNK
    quarter = width // GROUP
    columns = own.shape[1]

    get_values = []
    for c in range(chunks):
        rows = pl.ds(c * CHUNK, CHUNK)
        source = proj_ref.at[0, rows, :]
        get_values.append(pltpu.make_async_copy(source, values_wide.at[rows, :], here_sem.at[c]))
        get_values[c].start()
    get_gates = pltpu.make_async_copy(proj_ref.at[1], gates, here_sem.at[chunks])
    get_weight = pltpu.make_async_copy(weight_hbm, weight_ref, here_sem.at[chunks + 1])
    get_gates.start()
    get_weight.start()

    def peer(zz, gg):
        return {"seq": zz * GROUP + gg}

    barrier = pltpu.get_barrier_semaphore()
    friends = [peer(z, (g + d) % GROUP) for d in range(1, GROUP)]
    friends += [peer((z + d) % outer, g) for d in range(1, outer)]
    friends += [{"tp": (me + d) % n} for d in range(1, n)]
    for friend in friends:
        pl.semaphore_signal(barrier, inc=1, device_id=friend, device_id_type=pl.DeviceIdType.MESH)

    def push(source, target, sends, recvs, slot, where):
        copy = pltpu.make_async_remote_copy(
            src_ref=source,
            dst_ref=target,
            send_sem=sends.at[slot],
            recv_sem=recvs.at[slot],
            device_id=where,
            device_id_type=pl.DeviceIdType.MESH,
        )
        copy.start()
        return copy

    every = chunks * heads2
    raw = jnp.concatenate(
        [raw_ref[c * CHUNK : (c + 1) * CHUNK, :] for c in range(chunks)], axis=1
    )
    rate = jnp.concatenate([rate_ref[...]] * (2 * chunks), axis=1)
    steps = jnp.maximum(raw, 0.0) + jnp.log1p(jnp.exp(-jnp.abs(raw)))
    logs = -rate * steps
    rows_of = lax.broadcasted_iota(jnp.int32, (CHUNK, CHUNK), 0)
    cols_of = lax.broadcasted_iota(jnp.int32, (CHUNK, CHUNK), 1)
    upto = dot((rows_of >= cols_of).astype(F32), logs, precision=HIGH)
    before = upto - logs
    last = upto[CHUNK - 1 : CHUNK, :]
    forward = lax.rem(lax.broadcasted_iota(jnp.int32, (CHUNK, every), 1), heads2) < heads
    weight = jnp.exp(jnp.where(forward, last - upto, before)) * steps
    column = LOG2_E * jnp.where(forward, before, -upto)
    row = (LOG2_E * (jnp.where(forward, -upto, before) + jnp.log(steps))).T
    scale = jnp.exp(jnp.where(forward, before, last - upto))
    lasts = [last[:, c * heads2 : (c + 1) * heads2] for c in range(chunks)]
    passed = []
    for c in range(chunks):
        gone = jnp.zeros((1, heads2), F32)
        for other in range(chunks):
            if other < c:
                gone = gone + jnp.where(forward[:1, :heads2], lasts[other], 0.0)
            if other > c:
                gone = gone + jnp.where(forward[:1, :heads2], 0.0, lasts[other])
        passed.append(gone)
    enter_scale = scale * jnp.exp(jnp.concatenate(passed, axis=1))
    spread = spread_matrix(heads2, BF16, 2)
    spread_one = spread_matrix(heads, BF16, 2)
    stack = lasts + [functools.reduce(jnp.add, lasts)]
    stack = stack + [jnp.zeros((1, heads2), F32)] * (8 - len(stack))
    totals = dot(jnp.concatenate(stack, axis=0), spread_matrix(heads2, F32), precision=HIGH)
    gain = jnp.broadcast_to(gain_ref[...], (8, heads))
    gain = dot(gain, spread_matrix(heads, F32), precision=HIGH)[:1]

    def spread_chunk(value, c):
        return dot(split_wide(value[:, c * heads2 : (c + 1) * heads2]), spread)

    for c in range(chunks):
        get_values[c].wait()
        rows = slice(c * CHUNK, (c + 1) * CHUNK)
        values = values_wide[rows, :].astype(BF16).astype(F32)
        wide = jnp.concatenate([values, values], axis=1) * spread_chunk(weight, c)
        weighted[c] = wide.astype(BF16)
        turned[c] = both_ref[rows, :STATE].T

    def block_state(rows):
        for way in range(2):
            side = slice(way * width, (way + 1) * width)
            carry = jnp.zeros((rows.stop - rows.start, width), F32)
            for c in range(chunks) if way == 0 else range(chunks - 1, -1, -1):
                local[c, rows, side] = carry.astype(BF16)
                new = dot(turned[c, rows, :], weighted[c, :, side])
                carry = jnp.exp(totals[c : c + 1, side]) * carry + new
            for q in range(GROUP):
                part = slice(q * quarter, (q + 1) * quarter)
                send_ref[q, way, rows, :] = carry[:, part].astype(BF16)

    for way in range(2):
        for q in range(GROUP):
            part = slice(way * width + q * quarter, way * width + (q + 1) * quarter)
            total_ref[q, way] = jnp.broadcast_to(totals[chunks : chunks + 1, part], (8, quarter))

    bands = [pl.ds(p * (STATE // PARTS), STATE // PARTS) for p in range(PARTS)]
    first = [[] for _ in bands]
    second = [[] for _ in bands]
    third = []
    before_state = [[None] * GROUP, [None] * GROUP]

    def share(p):
        for d in range(1, GROUP):
            to = (g + d) % GROUP
            if p == 0:
                total = total_ref.at[to]
                first[p].append(push(total, got_total.at[g], send1, recv1, d - 1, peer(z, to)))
            slot = (p + 1) * (GROUP - 1) + d - 1
            source = send_ref.at[to, :, bands[p], :]
            target = got.at[g, :, bands[p], :]
            first[p].append(push(source, target, send1, recv1, slot, peer(z, to)))

    def along(p):
        band = bands[p]
        for copy in first[p]:
            copy.wait()
        for way in range(2):
            carry = jnp.zeros((STATE // PARTS, quarter), F32)
            gone = jnp.zeros((8, quarter), F32)
            for s in range(GROUP) if way == 0 else range(GROUP - 1, -1, -1):
                inner[s, way, band, :] = carry
                before_state[way][s] = jnp.exp(gone[:1])
                carry = jnp.exp(got_total[s, way][:1]) * carry + got[s, way, band, :].astype(F32)
                gone = gone + got_total[s, way]
            group[way, band, :] = carry.astype(BF16)
            if p == 0:
                group_total[way] = gone
        for d in range(1, outer):
            way = (z + d) // outer
            to = peer((z + d) % outer, g)
            if p == 0:
                total = group_total.at[way]
                second[p].append(push(total, far_total.at[z], send2, recv2, d - 1, to))
            slot = (p + 1) * (outer - 1) + d - 1
            source = group.at[way, band, :]
            second[p].append(push(source, far.at[z, band, :], send2, recv2, slot, to))

    def hand_back(p):
        band = bands[p]
        for copy in second[p]:
            copy.wait()
        for way in range(2):
            carry = jnp.zeros((STATE // PARTS, quarter), F32)
            for s in range(outer) if way == 0 else range(outer - 1, -1, -1):
                longer = jnp.exp(far_total[s][:1]) * carry + far[s, band, :].astype(F32)
                carry = jnp.where(s < z if way == 0 else s > z, longer, carry)
            for s in range(GROUP):
                entering = inner[s, way, band, :] + before_state[way][s] * carry
                back[s, way, band, :] = entering.astype(BF16)
        for d in range(1, GROUP):
            to = (g + d) % GROUP
            slot = p * (GROUP - 1) + d - 1
            source = back.at[to, :, band, :]
            third.append(push(source, landed.at[g, :, band, :], send3, recv3, slot, peer(z, to)))

    half = STATE // 2
    block_state(slice(0, half))
    pl.semaphore_wait(barrier, GROUP - 1 + outer - 1 + n - 1)
    share(0)
    share(1)
    block_state(slice(half, STATE))
    share(2)
    share(3)
    got[g] = send_ref[g]
    got_total[g] = total_ref[g]
    far[z] = jnp.zeros(far.shape[1:], BF16)
    far_total[z] = jnp.zeros(far_total.shape[1:], F32)

    lower = rows_of > cols_of
    on_line = rows_of == cols_of
    first_half = lax.broadcasted_iota(jnp.int32, (CHUNK, 2 * HEAD_DIM), 1) < HEAD_DIM

    def inside(c):
        rows = slice(c * CHUNK, (c + 1) * CHUNK)
        scores = dot(both_ref[rows, STATE:], both_ref[rows, :STATE], ((1,), (1,)))
        for pair in range(heads // 2):
            weights = []
            for h in (2 * pair, 2 * pair + 1):
                f = c * heads2 + h
                b = f + heads
                power = jnp.where(
                    lower,
                    column[:, f : f + 1] + row[f : f + 1, :],
                    column[:, b : b + 1] + row[b : b + 1, :],
                )
                power = jnp.where(on_line, -jnp.inf, power)
                weights.append((scores * jnp.exp2(power)).astype(BF16))
            lanes = slice(pair * 2 * HEAD_DIM, (pair + 1) * 2 * HEAD_DIM)
            pair_values = values_wide[rows, lanes].astype(BF16)
            zero = jnp.zeros_like(pair_values)
            stacked = jnp.concatenate(
                [
                    jnp.where(first_half, pair_values, zero),
                    jnp.where(first_half, zero, pair_values),
                ],
                axis=0,
            )
            mix[rows, lanes] = dot(jnp.concatenate(weights, axis=1), stacked)

    def nearby(c):
        rows = slice(c * CHUNK, (c + 1) * CHUNK)
        reach = dot(both_ref[rows, STATE:], local[c]) * spread_chunk(scale, c)
        values = values_wide[rows, :].astype(BF16).astype(F32)
        mix[rows, :] = mix[rows, :] + reach[:, :width] + reach[:, width:] + gain * values

    def activate(c):
        rows = slice(c * CHUNK, (c + 1) * CHUNK)
        gates[rows, :] = gates[rows, :] / (1.0 + jnp.exp(-gates[rows, :]))

    def spread_scale(c):
        scales[c] = spread_chunk(enter_scale, c)

    inside(0)
    along(0)
    along(1)
    inside(1)
    along(2)
    along(3)
    hand_back(0)
    inside(2)
    hand_back(1)
    hand_back(2)
    inside(3)
    hand_back(3)
    landed[g] = back[g]
    get_gates.wait()
    for c in range(chunks):
        nearby(c)
        activate(c)
        spread_scale(c)
    get_weight.wait()
    for copy in third:
        copy.wait()

    copies = []
    for c in range(chunks):
        rows = slice(c * CHUNK, (c + 1) * CHUNK)
        queries = both_ref[rows, STATE:]
        reach = [dot(queries, landed[q, way]) for way in range(2) for q in range(GROUP)]
        reach = jnp.concatenate(reach, axis=1) * scales[c]
        gated = (mix[rows, :] + reach[:, :width] + reach[:, width:]) * gates[rows, :]
        square = gated * gated
        high = square.astype(BF16)
        low = (square - high.astype(F32)).astype(BF16)
        unit = spread_one[:heads]
        power = dot(high, unit, ((1,), (1,))) + dot(low, unit, ((1,), (1,)))
        norm = lax.rsqrt(power * (1.0 / HEAD_DIM) + 1e-05)
        hidden[rows, :] = (gated * dot(split_wide(norm), spread_one)).astype(BF16)
        if c % 2 == 0:
            continue
        rows = slice((c - 1) * CHUNK, (c + 1) * CHUNK)
        for d in range(1, n):
            to = (me + d) % n
            theirs = pl.ds(pl.multiple_of(to * columns, columns), columns)
            leaving[d - 1, rows, :] = dot(hidden[rows, :], weight_ref[:, theirs]).astype(BF16)
            slot = c // 2 * (n - 1) + d - 1
            source = leaving.at[d - 1, rows, :]
            copies.append(
                push(source, arrived.at[d - 1, rows, :], send4, recv4, slot, {"tp": to})
            )
    mine = pl.ds(pl.multiple_of(me * columns, columns), columns)
    own[...] = dot(hidden[...], weight_ref[:, mine]).astype(BF16)
    for copy in copies:
        copy.wait()


def shards(tokens, in_weight, bc_weight, dt_weight, dt_bias, decay_rate, skip_gain, out_weight):
    heads = decay_rate.shape[0]
    width = heads * HEAD_DIM
    quarter = width // GROUP
    outer = lax.axis_size("seq") // GROUP
    n = lax.axis_size("tp")
    length = tokens.shape[0]
    features = dt_weight.shape[1]
    chunks = length // CHUNK
    columns = out_weight.shape[1] // n
    vmem = pl.BlockSpec(memory_space=pltpu.VMEM)
    anywhere = pl.BlockSpec(memory_space=pl.ANY)
    dma = pltpu.SemaphoreType.DMA
    whole, both, raw = pl.pallas_call(
        functools.partial(gather_kernel, n),
        out_shape=(
            jax.ShapeDtypeStruct((length, features), BF16),
            jax.ShapeDtypeStruct((length, 2 * STATE), BF16),
            jax.ShapeDtypeStruct((length, 2 * heads), F32),
        ),
        in_specs=[pl.BlockSpec(memory_space=pltpu.HBM)] * 3 + [vmem],
        out_specs=(anywhere, vmem, vmem),
        scratch_shapes=[
            pltpu.VMEM((n,) + bc_weight.shape, BF16),
            pltpu.VMEM((2 * heads, features), BF16),
            pltpu.VMEM(tokens.shape, BF16),
            pltpu.VMEM((n - 1,) + tokens.shape, BF16),
        ]
        + [dma((n - 1,))] * 2
        + [dma((2 * (n - 1),))] * 2
        + [dma((4,)), dma((2 * (n - 1),))],
        compiler_params=pltpu.CompilerParams(
            vmem_limit_bytes=GATHER_LIMIT, collective_id=0, has_side_effects=True
        ),
        name="gather_features",
    )(
        tokens,
        bc_weight,
        dt_weight.transpose(0, 2, 1).reshape(2 * heads, features),
        dt_bias,
    )
    projected = jnp.einsum("td,dkf->ktf", whole, in_weight, preferred_element_type=F32)
    own, arrived = pl.pallas_call(
        functools.partial(mixer_kernel, outer, n),
        out_shape=(
            jax.ShapeDtypeStruct((length, columns), BF16),
            jax.ShapeDtypeStruct((n - 1, length, columns), BF16),
        ),
        in_specs=[anywhere, vmem, vmem, vmem, vmem, anywhere],
        out_specs=(vmem, vmem),
        scratch_shapes=[
            pltpu.VMEM((length, width), F32),
            pltpu.VMEM((length, width), F32),
            pltpu.VMEM(out_weight.shape, BF16),
            pltpu.VMEM((chunks, CHUNK, 2 * width), BF16),
            pltpu.VMEM((chunks, STATE, CHUNK), BF16),
            pltpu.VMEM((chunks, STATE, 2 * width), BF16),
            pltpu.VMEM((length, width), F32),
            pltpu.VMEM((GROUP, 2, STATE, quarter), BF16),
            pltpu.VMEM((GROUP, 2, 8, quarter), F32),
            pltpu.VMEM((GROUP, 2, STATE, quarter), BF16),
            pltpu.VMEM((GROUP, 2, 8, quarter), F32),
            pltpu.VMEM((GROUP, 2, STATE, quarter), F32),
            pltpu.VMEM((2, STATE, quarter), BF16),
            pltpu.VMEM((2, 8, quarter), F32),
            pltpu.VMEM((outer, STATE, quarter), BF16),
            pltpu.VMEM((outer, 8, quarter), F32),
            pltpu.VMEM((GROUP, 2, STATE, quarter), BF16),
            pltpu.VMEM((GROUP, 2, STATE, quarter), BF16),
            pltpu.VMEM((length, width), BF16),
            pltpu.VMEM((chunks, CHUNK, 2 * width), F32),
            pltpu.VMEM((n - 1, length, columns), BF16),
        ]
        + [dma(((PARTS + 1) * (GROUP - 1),))] * 2
        + [dma(((PARTS + 1) * (outer - 1),))] * 2
        + [dma((PARTS * (GROUP - 1),))] * 2
        + [dma((chunks // 2 * (n - 1),))] * 2
        + [dma((chunks + 2,))],
        compiler_params=pltpu.CompilerParams(
            vmem_limit_bytes=VMEM_LIMIT, collective_id=1, has_side_effects=True
        ),
        name="mixer",
    )(projected, both, raw, decay_rate[None], skip_gain[None], out_weight)
    total = own.astype(F32)
    for d in range(n - 1):
        total = total + arrived[d].astype(F32)
    return total.astype(BF16)


def solution(mesh):
    in_specs = (
        P("seq", "tp"),
        P(None, None, "tp"),
        P(None, "tp"),
        P(None, None, "tp"),
        P(None, "tp"),
        P("tp"),
        P("tp"),
        P("tp", None),
    )
    out_specs = P("seq", "tp")
    return jax.shard_map(shards, mesh=mesh, in_specs=in_specs, out_specs=out_specs, check_vma=False)
```
